256 devices in a mesh: row: 32 (over z, x_lo, core), col: 8 (over x_hi, y).
Axes of the slice: x: 4 (x_hi: 2, x_lo: 2; x = x_hi * 2 + x_lo), y: 4, z: 8, core: 2. Of those that a mesh axis runs over, the one named last changes fastest.
Arguments:
- pair_in: bfloat16 [64, 1024, 1024], P(None, 'row', 'col'), may hold values from -6 to 6
- row_feat: bfloat16 [64, 1024], P('col', 'row'), may hold values from -4 to 4
- col_feat: bfloat16 [64, 1024], P('row', 'col'), may hold values from -4 to 4
- cotangent: bfloat16 [64, 1024, 1024], P(None, 'row', 'col'), may hold values from -6 to 6
- conv_weight: bfloat16 [9, 64, 64], replicated, may hold values from -0.25 to 0.25
- norm_gain: float32 [64], replicated, may hold values from 0.25 to 1.75
- norm_shift: float32 [64], replicated, may hold values from -1 to 1
- proj_weight: bfloat16 [64, 64], replicated, may hold values from -0.75 to 0.75
Outputs:
- pair_grad: bfloat16 [64, 1024, 1024], P(None, 'row', 'col')
- row_grad: float32 [64, 1024], P('col', 'row')
- col_grad: float32 [64, 1024], P('row', 'col')
- conv_grad: float32 [9, 64, 64], replicated
- proj_grad: float32 [64, 64], replicated
- gain_grad: float32 [64], replicated
- shift_grad: float32 [64], replicated
The draws below stay inside these ranges and needn't reach their ends.
All inputs are finite; a program needn't handle non-finite values.
Results may differ from the reference program's by a relative error of at most 0.019.
Values may be sent and summed in bfloat16 or wider, within the bound.
A program may use at most 64 MiB of HBM per device.

```python
import math
import jax
import jax.numpy as jnp
from jax import lax

CHANNELS = 64
DILATION = 8
ROW_DEV = 32
BINS = 1024
N_ROW = 32


def block_levels(key, dims, split, low, largest):
    level = 1.0
    for axis_at, parts in split:
        heights = jax.random.uniform(jax.random.fold_in(jax.random.fold_in(key, 6), axis_at), (parts,), jnp.float32, low / len(split), largest / len(split))
        level = level * jnp.repeat(jnp.exp(heights), dims[axis_at] // parts).reshape((-1,) + (1,) * (len(dims) - 1 - axis_at))
    return level


def scatter_about(stream_key, dims, scale, limit, split=(), held_as=jnp.bfloat16):
    gain = block_levels(stream_key, dims, split, -0.22, 0.18) if split else 1.0
    entries = jax.random.normal(stream_key, dims, jnp.float32) * scale * gain
    return jnp.minimum(jnp.maximum(entries, -limit), limit).astype(held_as)


def setup_inputs(seed: int = 0) -> dict:
    keys = jax.random.split(jax.random.key(seed), 9)
    return {
        "pair_in": scatter_about(keys[0], (CHANNELS, BINS, BINS), 1.0, 6.0, ((1, 32), (2, 8))),
        "row_feat": scatter_about(keys[1], (CHANNELS, BINS), 0.5, 4.0, ((0, 8), (1, 32))),
        "col_feat": scatter_about(keys[2], (CHANNELS, BINS), 0.5, 4.0, ((0, 32), (1, 8))),
        "cotangent": scatter_about(keys[3], (CHANNELS, BINS, BINS), 1.0, 6.0, ((1, 32), (2, 8))),
        "conv_weight": scatter_about(keys[4], (9, CHANNELS, CHANNELS), (9 * CHANNELS) ** -0.5, 0.25),
        "norm_gain": jnp.clip(1.0 + 0.15 * jax.random.normal(keys[5], (CHANNELS,), jnp.float32), 0.25, 1.75),
        "norm_shift": jnp.clip(jax.random.uniform(keys[6], (CHANNELS,), jnp.float32, -1.0, 1.0), -1.0, 1.0),
        "proj_weight": scatter_about(keys[7], (CHANNELS, CHANNELS), CHANNELS ** -0.5, 0.75),
    }


def dilated(padded, conv_weight, out_rows, out_cols):
    summed = jnp.zeros((conv_weight.shape[1], out_rows, out_cols), jnp.float32)
    for tap_row in range(3):
        for tap_col in range(3):
            window = padded[:, tap_row * DILATION:tap_row * DILATION + out_rows, tap_col * DILATION:tap_col * DILATION + out_cols]
            summed = summed + jnp.einsum('oc,crw->orw', conv_weight[3 * tap_row + tap_col].astype(jnp.float32), window.astype(jnp.float32), precision=lax.Precision.HIGHEST)
    return summed

def transposed(padded, conv_weight, out_rows, out_cols):
    summed = jnp.zeros((conv_weight.shape[2], out_rows, out_cols), jnp.float32)
    for tap_row in range(3):
        for tap_col in range(3):
            first = (2 - tap_row) * DILATION
            second = (2 - tap_col) * DILATION
            window = padded[:, first:first + out_rows, second:second + out_cols]
            summed = summed + jnp.einsum('oc,orw->crw', conv_weight[3 * tap_row + tap_col].astype(jnp.float32), window.astype(jnp.float32), precision=lax.Precision.HIGHEST)
    return summed

def weight_grad(own_grad, padded, out_rows, out_cols, offset):
    result = []
    for tap_row in range(3):
        for tap_col in range(3):
            first = offset + tap_row * DILATION
            second = offset + tap_col * DILATION
            window = padded[:, first:first + out_rows, second:second + out_cols]
            result.append(jnp.einsum('orw,crw->oc', own_grad.astype(jnp.float32), window.astype(jnp.float32), precision=lax.Precision.HIGHEST))
    return jnp.stack(result)

def reference(pair_in, row_feat, col_feat, cotangent, conv_weight, norm_gain, norm_shift, proj_weight):
    pre = pair_in.astype(jnp.float32) + row_feat.astype(jnp.float32)[:, :, None] + col_feat.astype(jnp.float32)[:, None, :]
    active = jnp.maximum(pre, 0.0).astype(jnp.bfloat16)
    margin = ((0, 0), (DILATION, DILATION), (DILATION, DILATION))
    act_pad = jnp.pad(active, margin)
    gain_col = norm_gain[:, None, None]
    shift_col = norm_shift[:, None, None]
    indices = jnp.arange(N_ROW, dtype=jnp.int32)

    def first_pass(index):
        start = (index * ROW_DEV).astype(jnp.int32)
        window = lax.dynamic_slice_in_dim(act_pad, start, ROW_DEV + 2 * DILATION, 1)
        upstream = lax.dynamic_slice_in_dim(cotangent, start, ROW_DEV, 1)
        conv_out = dilated(window, conv_weight, ROW_DEV, BINS)
        normed = gain_col * conv_out + shift_col
        sig = jax.nn.sigmoid(normed)
        hidden = (normed * sig).astype(jnp.bfloat16)
        back = jnp.einsum('oc,orw->crw', proj_weight.astype(jnp.float32), upstream.astype(jnp.float32), precision=lax.Precision.HIGHEST)
        normed_grad = back * sig * (1.0 + normed * (1.0 - sig))
        conv_out_grad = (gain_col * normed_grad).astype(jnp.bfloat16)
        proj_part = jnp.einsum('orw,crw->oc', upstream.astype(jnp.float32), hidden.astype(jnp.float32), precision=lax.Precision.HIGHEST)
        return (conv_out_grad, proj_part, lax.optimization_barrier(jnp.sum(normed_grad * conv_out, axis=(1, 2))), lax.optimization_barrier(jnp.sum(normed_grad, axis=(1, 2))))
    grads, proj_parts, gain_parts, shift_parts = lax.map(first_pass, indices)
    conv_out_grad = jnp.moveaxis(grads, 0, 1).reshape(CHANNELS, BINS, BINS)
    grad_pad = jnp.pad(conv_out_grad, margin)

    def second_pass(index):
        start = (index * ROW_DEV).astype(jnp.int32)
        grad_window = lax.dynamic_slice_in_dim(grad_pad, start, ROW_DEV + 2 * DILATION, 1)
        own_grad = grad_window[:, DILATION:DILATION + ROW_DEV, DILATION:DILATION + BINS]
        act_window = lax.dynamic_slice_in_dim(act_pad, start, ROW_DEV + 2 * DILATION, 1)
        pre_block = lax.dynamic_slice_in_dim(pre, start, ROW_DEV, 1)
        upstream = lax.dynamic_slice_in_dim(cotangent, start, ROW_DEV, 1)
        act_grad = transposed(grad_window, conv_weight, ROW_DEV, BINS)
        pre_grad = jnp.where(pre_block > 0, act_grad, 0.0)
        pair_block = (upstream.astype(jnp.float32) + pre_grad).astype(jnp.bfloat16)
        conv_part = weight_grad(own_grad, act_window, ROW_DEV, BINS, 0)
        return (pair_block, lax.optimization_barrier(jnp.sum(pre_grad, axis=2)), lax.optimization_barrier(jnp.sum(pre_grad, axis=1)), conv_part)
    pair_blocks, row_parts, col_parts, conv_parts = lax.map(second_pass, indices)
    pair_grad = jnp.moveaxis(pair_blocks, 0, 1).reshape(CHANNELS, BINS, BINS)
    root = math.sqrt(BINS)
    row_grad = jnp.moveaxis(row_parts, 0, 1).reshape(CHANNELS, BINS) / root
    col_grad = lax.optimization_barrier(jnp.sum(col_parts, axis=0)) / root
    conv_grad = lax.optimization_barrier(jnp.sum(conv_parts, axis=0)) / BINS
    proj_grad = lax.optimization_barrier(jnp.sum(proj_parts, axis=0)) / BINS
    gain_grad = lax.optimization_barrier(jnp.sum(gain_parts, axis=0)) / BINS
    shift_grad = lax.optimization_barrier(jnp.sum(shift_parts, axis=0)) / BINS
    return (pair_grad, row_grad, col_grad, conv_grad, proj_grad, gain_grad, shift_grad)
```

```python
import functools
import math

import jax
import jax.numpy as jnp
from jax import lax
from jax.experimental import pallas as pl
from jax.experimental.pallas import tpu as pltpu
from jax.sharding import PartitionSpec as P

C = 64
D = 8
TR = 32
TC = 128
PR = TR + 2 * D
LANES = PR * TC
OWN = D * TC
TILE = TR * TC
F32 = jnp.float32
BF16 = jnp.bfloat16
MESH = pl.DeviceIdType.MESH


def dot(a, b):
    return lax.dot_general(a, b, (((1,), (0,)), ((), ())), preferred_element_type=F32)


def dot_nt(a, b):
    return lax.dot_general(a, b, (((1,), (1,)), ((), ())), preferred_element_type=F32)


def kernel(
    nr,
    nc,
    pair_ref,
    rowf_ref,
    colf_ref,
    cot_ref,
    w_ref,
    gain_ref,
    shift_ref,
    proj_ref,
    pg_ref,
    rowg_ref,
    colg_ref,
    convg_ref,
    projg_ref,
    gaing_ref,
    shiftg_ref,
    xs,
    cs,
    wf,
    wd,
    gainb,
    shiftb,
    rf,
    cf,
    cfull,
    s2,
    c2,
    pkl,
    pkr,
    hl,
    hr,
    cv,
    bk,
    gz,
    g2,
    qkl,
    qkr,
    kl,
    kr,
    gacc,
    sacc,
    wacc,
    rs_send,
    rs_recv,
    zb,
    ag,
    cacc,
    racc,
    cgs,
    cgr,
    rgs,
    rgr,
    feat_sems,
    halo_send,
    halo_recv,
    grad_send,
    grad_recv,
    red_sems,
    out_sems,
):
    row = lax.axis_index("row")
    col = lax.axis_index("col")
    nz = nr // 4
    na = 4 * nc
    cr = 256 // na
    cpr = C // nr
    cpc = C // nc
    zi = row // 4
    ai = lax.rem(row, 4) * nc + col
    up, down = lax.rem(row + nr - 1, nr), lax.rem(row + 1, nr)
    left, right = lax.rem(col + nc - 1, nc), lax.rem(col + 1, nc)
    bins = TR * nr

    def row_peer(k):
        return (lax.rem(row + k, nr), col)

    def col_peer(k):
        return (row, lax.rem(col + k, nc))

    def a_peer(k):
        idx = lax.rem(ai + k, na)
        return (zi * 4 + idx // nc, lax.rem(idx, nc))

    def z_peer(k):
        return (lax.rem(zi + k, nz) * 4 + lax.rem(row, 4), col)

    barrier = pltpu.get_barrier_semaphore()

    def greet(peer, count):
        def body(k, _):
            pl.semaphore_signal(barrier, inc=1, device_id=peer(k), device_id_type=MESH)
            return 0

        lax.fori_loop(1, count, body, 0)

    greet(row_peer, nr)
    greet(a_peer, na)
    for dr in (up, down):
        for dc in (left, right):
            pl.semaphore_signal(barrier, inc=1, device_id=(dr, dc), device_id_type=MESH)

    lane = lax.broadcasted_iota(jnp.int32, (C, TC), 1)

    rf[col] = jnp.concatenate(
        [rowf_ref[...].astype(F32), jnp.zeros((cpc, TC - TR), F32)], axis=1
    )
    cf[row] = colf_ref[...].astype(F32)
    for i in range(8):
        xs[pl.ds(i * 256, 256), :] = pair_ref[pl.ds(i * 8, 8)].astype(F32).reshape(256, TC)
        cs[pl.ds(i * 256, 256), :] = cot_ref[pl.ds(i * 8, 8)].astype(F32).reshape(256, TC)

    wf[...] = jnp.zeros_like(wf)
    for p in range(3):
        wf[pl.ds(C * p, C), :] = jnp.concatenate(
            [w_ref[3 * p], w_ref[3 * p + 1], w_ref[3 * p + 2], jnp.zeros((C, C), BF16)], axis=1
        )
    wf[pl.ds(3 * C, C), :] = jnp.concatenate(
        [jnp.zeros((C, 3 * C), BF16), proj_ref[...].astype(F32).T.astype(BF16)], axis=1
    )
    for q in range(3):
        stacked = jnp.concatenate(
            [w_ref[3 * (2 - p) + 2 - q].astype(F32).T for p in range(3)], axis=0
        )
        wd[:, pl.ds(C * q, C)] = stacked.astype(BF16)
    eye = lax.broadcasted_iota(jnp.int32, (C, C), 0) == lax.broadcasted_iota(jnp.int32, (C, C), 1)
    for src, dst in ((gain_ref, gainb), (shift_ref, shiftb)):
        column = jnp.sum(jnp.where(eye, src[...], 0.0), axis=1, keepdims=True)
        dst[...] = jnp.broadcast_to(column, (C, 2 * TC))

    for r in range(TR):
        c2[:, pl.ds(OWN + r * TC, TC)] = cs[pl.ds(r, C, stride=TR), :].astype(BF16)
    zeros = jnp.zeros((C, OWN), BF16)
    for part in (0, PR - D):
        c2[:, pl.ds(part * TC, OWN)] = zeros
        s2[pl.ds(3 * C, C), pl.ds(part * TC, OWN)] = zeros
    s2[pl.ds(3 * C, C), pl.ds(OWN, TILE)] = c2[:, pl.ds(OWN, TILE)]
    for part in (0, 1, 6, 7):
        gz[:, pl.ds(part * OWN, OWN)] = zeros

    pl.semaphore_wait(barrier, (nr - 1) + (na - 1) + 4)

    def rf_copy(k):
        return pltpu.make_async_remote_copy(
            rf.at[col], rf.at[col], feat_sems.at[0], feat_sems.at[1], col_peer(k), MESH
        )

    def cf_copy(k):
        return pltpu.make_async_remote_copy(
            cf.at[row], cf.at[row], feat_sems.at[2], feat_sems.at[3], row_peer(k), MESH
        )

    def start_all(copy, count):
        def body(k, _):
            copy(k).start()
            return 0

        lax.fori_loop(1, count, body, 0)

    def wait_bytes(ref, sem):
        pltpu.make_async_copy(ref, ref, sem).wait()

    start_all(rf_copy, nc)
    start_all(cf_copy, nr)
    wait_bytes(rf.at[pl.ds(0, nc - 1)], feat_sems.at[1])
    wait_bytes(cf.at[pl.ds(0, nr - 1)], feat_sems.at[3])

    for i in range(nr):
        cfull[pl.ds(i * cpr, cpr), :] = cf[i]
    row_full = rf[...].reshape(C, TC)
    col_full = cfull[...]

    def packed(parts, edge):
        result = jnp.zeros((C, TC), F32)
        for k, x in enumerate(parts):
            shift = (8 * k + edge) % TC
            moved = pltpu.roll(x, shift, 1) if shift else x
            result = jnp.where(lane // 8 == k, moved, result)
        return result.astype(BF16)

    for b in range(2):
        parts = []
        for k in range(16):
            r = 16 * b + k
            pre = xs[pl.ds(r, C, stride=TR), :] + row_full[:, r : r + 1] + col_full
            act = jnp.maximum(pre, 0.0)
            s2[pl.ds(C, C), pl.ds(OWN + r * TC, TC)] = act.astype(BF16)
            parts.append(act)
        pkl[b] = packed(parts, 0)
        pkr[b] = packed(parts, 8)

    def halo_copies(center_src, src_base, center_dst, lsend, rsend, lrecv, rrecv, ssem, rsem):
        plan = (
            (center_src(src_base, OWN), center_dst(OWN + TILE, OWN), (up, col)),
            (center_src(src_base + TILE - OWN, OWN), center_dst(0, OWN), (down, col)),
            (lsend, rrecv.at[pl.ds(1, 2)], (row, left)),
            (rsend, lrecv.at[pl.ds(1, 2)], (row, right)),
            (lsend.at[0], rrecv.at[3], (up, left)),
            (lsend.at[1], rrecv.at[0], (down, left)),
            (rsend.at[0], lrecv.at[3], (up, right)),
            (rsend.at[1], lrecv.at[0], (down, right)),
        )
        return [
            pltpu.make_async_remote_copy(src, dst, ssem.at[i], rsem.at[i], device, MESH)
            for i, (src, dst, device) in enumerate(plan)
        ]

    def clear_edges(center, lrecv, rrecv):
        @pl.when(row == 0)
        def _():
            center[pl.ds(C, C), pl.ds(0, OWN)] = jnp.zeros((C, OWN), BF16)
            lrecv[0] = jnp.zeros((C, TC), BF16)
            rrecv[0] = jnp.zeros((C, TC), BF16)

        @pl.when(row == nr - 1)
        def _():
            center[pl.ds(C, C), pl.ds(OWN + TILE, OWN)] = jnp.zeros((C, OWN), BF16)
            lrecv[3] = jnp.zeros((C, TC), BF16)
            rrecv[3] = jnp.zeros((C, TC), BF16)

        @pl.when(col == 0)
        def _():
            lrecv[...] = jnp.zeros_like(lrecv)

        @pl.when(col == nc - 1)
        def _():
            rrecv[...] = jnp.zeros_like(rrecv)

    def build_shifts(center, lrecv, rrecv):
        for b in range(4):
            lo = lrecv[b].astype(F32)
            hi = rrecv[b].astype(F32)
            for k in range(16):
                r = 16 * b + k - 8
                if not 0 <= r < PR:
                    continue
                x = center[pl.ds(C, C), pl.ds(r * TC, TC)].astype(F32)
                from_left = pltpu.roll(lo, (TC - 8 * k) % TC, 1) if k else lo
                from_right = pltpu.roll(hi, 120 - 8 * k, 1) if k < 15 else hi
                center[pl.ds(0, C), pl.ds(r * TC, TC)] = jnp.where(
                    lane < 8, from_left, pltpu.roll(x, 8, 1)
                ).astype(BF16)
                center[pl.ds(2 * C, C), pl.ds(r * TC, TC)] = jnp.where(
                    lane >= 120, from_right, pltpu.roll(x, 120, 1)
                ).astype(BF16)

    def center_of(ref):
        return lambda base, size: ref.at[pl.ds(C, C), pl.ds(base, size)]

    copies = halo_copies(
        center_of(s2), OWN, center_of(s2), pkl, pkr, hl, hr, halo_send, halo_recv
    )
    for copy in copies:
        copy.start()
    for copy in copies:
        copy.wait_recv()
    clear_edges(s2, hl, hr)
    build_shifts(s2, hl, hr)

    def at(i, size=256):
        return pl.ds(pl.multiple_of(i * 256, 256), size)

    def forward(i, _):
        out = dot(wf[...], s2[:, at(i)])
        cv[:, at(i + 8)] = out[:C]
        cv[:, at(i + 4)] += out[C : 2 * C]
        cv[:, at(i)] += out[2 * C : 3 * C]
        bk[:, at(i)] = out[3 * C :]
        return 0

    lax.fori_loop(0, PR // 2, forward, 0)

    gacc[...] = jnp.zeros_like(gacc)
    sacc[...] = jnp.zeros_like(sacc)

    def head(i, _):
        conv_out = cv[:, at(i + 8)]
        gain = gainb[...]
        normed = gain * conv_out + shiftb[...]
        sigma = jax.nn.sigmoid(normed)
        s2[pl.ds(3 * C, C), at(i + 4)] = (normed * sigma).astype(BF16)
        normed_grad = bk[:, at(i + 4)] * sigma * (1.0 + normed * (1.0 - sigma))
        gacc[...] += normed_grad * conv_out
        sacc[...] += normed_grad
        grad = (gain * normed_grad).astype(BF16)
        gz[:, at(i + 8)] = grad
        g2[pl.ds(C, C), at(i + 4)] = grad
        return 0

    lax.fori_loop(0, TR // 2, head, 0)

    for b in range(2):
        parts = [
            gz[:, pl.ds(2 * OWN + (16 * b + k) * TC, TC)].astype(F32) for k in range(16)
        ]
        qkl[b] = packed(parts, 0)
        qkr[b] = packed(parts, 8)
    grad_copies = halo_copies(
        lambda base, size: gz.at[:, pl.ds(base, size)],
        2 * OWN,
        center_of(g2),
        qkl,
        qkr,
        kl,
        kr,
        grad_send,
        grad_recv,
    )
    for copy in grad_copies:
        copy.start()

    wacc[...] = jnp.zeros_like(wacc)

    def weights(i, _):
        base = i * 4
        lhs = jnp.concatenate(
            [
                gz[:, at(base + 8, 1024)],
                gz[:, at(base + 4, 1024)],
                gz[:, at(base, 1024)],
                c2[:, at(base, 1024)],
            ],
            axis=0,
        )
        wacc[...] += dot_nt(lhs, s2[:, at(base, 1024)])
        return 0

    lax.fori_loop(0, PR // 8, weights, 0)
    wacc[pl.ds(0, C), pl.ds(3 * C, 1)] = jnp.sum(gacc[...], axis=1, keepdims=True)
    wacc[pl.ds(0, C), pl.ds(3 * C + 1, 1)] = jnp.sum(sacc[...], axis=1, keepdims=True)

    for a in range(na):
        rs_send[a] = jnp.concatenate(
            [wacc[pl.ds(a * cr, cr), pl.ds(0, TC)], wacc[pl.ds(a * cr, cr), pl.ds(TC, TC)]], axis=0
        ).astype(BF16)

    def rs_copy(k):
        idx = lax.rem(ai + k, na)
        return pltpu.make_async_remote_copy(
            rs_send.at[idx], rs_recv.at[ai], red_sems.at[0], red_sems.at[1], a_peer(k), MESH
        )

    start_all(rs_copy, na)
    rs_recv[ai] = rs_send[ai]

    for copy in grad_copies:
        copy.wait_recv()
    clear_edges(g2, kl, kr)
    build_shifts(g2, kl, kr)

    def backward(i, _):
        out = dot(wd[...], g2[:, at(i)])
        cv[:, at(i + 8)] = out[:C]
        cv[:, at(i + 4)] += out[C : 2 * C]
        cv[:, at(i)] += out[2 * C :]
        return 0

    lax.fori_loop(0, PR // 2, backward, 0)

    wait_bytes(rs_recv.at[pl.ds(0, na - 1)], red_sems.at[1])
    zb[zi] = jnp.sum(rs_recv[...].astype(F32), axis=0)

    def z_copy(k):
        return pltpu.make_async_remote_copy(
            zb.at[zi], zb.at[zi], red_sems.at[2], red_sems.at[3], z_peer(k), MESH
        )

    start_all(z_copy, nz)

    root = math.sqrt(bins)
    col_sum = jnp.zeros((C, TC), F32)
    row_sum = jnp.zeros((C, TC), F32)
    for r in range(TR):
        act_grad = cv[:, pl.ds(2 * OWN + r * TC, TC)]
        active = s2[pl.ds(C, C), pl.ds(OWN + r * TC, TC)].astype(F32)
        pre_grad = jnp.where(active > 0, act_grad, 0.0)
        col_sum += pre_grad
        row_sum = jnp.where(lane == r, jnp.sum(pre_grad, axis=1, keepdims=True), row_sum)
        xs[pl.ds(r, C, stride=TR), :] = pre_grad + cs[pl.ds(r, C, stride=TR), :]
    cacc[...] = col_sum
    for i in range(nr):
        cgs[i] = cacc[pl.ds(i * cpr, cpr), :]
    rgs[...] = row_sum.reshape(nc, cpc, TC)

    def cg_copy(k):
        idx = lax.rem(row + k, nr)
        return pltpu.make_async_remote_copy(
            cgs.at[idx], cgr.at[row], out_sems.at[0], out_sems.at[1], row_peer(k), MESH
        )

    def rg_copy(k):
        idx = lax.rem(col + k, nc)
        return pltpu.make_async_remote_copy(
            rgs.at[idx], rgr.at[col], out_sems.at[2], out_sems.at[3], col_peer(k), MESH
        )

    start_all(cg_copy, nr)
    start_all(rg_copy, nc)
    cgr[row] = cgs[row]
    rgr[col] = rgs[col]

    wait_bytes(zb.at[pl.ds(0, nz - 1)], red_sems.at[3])
    ag[ai] = (jnp.sum(zb[...], axis=0) * (1.0 / bins)).astype(BF16)

    def ag_copy(k):
        return pltpu.make_async_remote_copy(
            ag.at[ai], ag.at[ai], red_sems.at[4], red_sems.at[5], a_peer(k), MESH
        )

    start_all(ag_copy, na)

    for i in range(8):
        pg_ref[pl.ds(i * 8, 8)] = xs[pl.ds(i * 256, 256), :].reshape(8, TR, TC).astype(BF16)

    wait_bytes(cgr.at[pl.ds(0, nr - 1)], out_sems.at[1])
    wait_bytes(rgr.at[pl.ds(0, nc - 1)], out_sems.at[3])
    colg_ref[...] = jnp.sum(cgr[...], axis=0) * (1.0 / root)
    rowg_ref[...] = jnp.sum(rgr[...], axis=0)[:, :TR] * (1.0 / root)

    wait_bytes(ag.at[pl.ds(0, na - 1)], red_sems.at[5])
    total = ag[...].astype(F32)
    low = total[:, :cr].reshape(256, TC)
    high = total[:, cr:].reshape(256, TC)
    for p in range(3):
        convg_ref[3 * p] = low[C * p : C * p + C, :C]
        convg_ref[3 * p + 1] = low[C * p : C * p + C, C:]
        convg_ref[3 * p + 2] = high[C * p : C * p + C, :C]
    projg_ref[...] = high[3 * C :, C:]
    gaing_ref[...] = jnp.sum(jnp.where(eye, high[:C, C : C + 1], 0.0), axis=0, keepdims=True)
    shiftg_ref[...] = jnp.sum(jnp.where(eye, high[:C, C + 1 : C + 2], 0.0), axis=0, keepdims=True)

    for copy in copies:
        copy.wait_send()
    for copy in grad_copies:
        copy.wait_send()
    wait_bytes(rf.at[pl.ds(0, nc - 1)], feat_sems.at[0])
    wait_bytes(cf.at[pl.ds(0, nr - 1)], feat_sems.at[2])
    wait_bytes(rs_send.at[pl.ds(0, na - 1)], red_sems.at[0])
    wait_bytes(zb.at[pl.ds(0, nz - 1)], red_sems.at[2])
    wait_bytes(ag.at[pl.ds(0, na - 1)], red_sems.at[4])
    wait_bytes(cgs.at[pl.ds(0, nr - 1)], out_sems.at[0])
    wait_bytes(rgs.at[pl.ds(0, nc - 1)], out_sems.at[2])


def shards(nr, nc, pair_in, row_feat, col_feat, cotangent, conv_weight, gain, shift, proj):
    na, nz = 4 * nc, nr // 4
    cr = 256 // na
    vmem = pl.BlockSpec(memory_space=pltpu.VMEM)
    scratch = dict(
        xs=pltpu.VMEM((C * TR, TC), F32),
        cs=pltpu.VMEM((C * TR, TC), F32),
        wf=pltpu.VMEM((4 * C, 4 * C), BF16),
        wd=pltpu.VMEM((3 * C, 3 * C), BF16),
        gainb=pltpu.VMEM((C, 2 * TC), F32),
        shiftb=pltpu.VMEM((C, 2 * TC), F32),
        rf=pltpu.VMEM((nc, C // nc, TC), F32),
        cf=pltpu.VMEM((nr, C // nr, TC), F32),
        cfull=pltpu.VMEM((C, TC), F32),
        s2=pltpu.VMEM((4 * C, LANES), BF16),
        c2=pltpu.VMEM((C, LANES), BF16),
        pkl=pltpu.VMEM((2, C, TC), BF16),
        pkr=pltpu.VMEM((2, C, TC), BF16),
        hl=pltpu.VMEM((4, C, TC), BF16),
        hr=pltpu.VMEM((4, C, TC), BF16),
        cv=pltpu.VMEM((C, LANES + 2 * OWN), F32),
        bk=pltpu.VMEM((C, LANES), F32),
        gz=pltpu.VMEM((C, LANES + 2 * OWN), BF16),
        g2=pltpu.VMEM((3 * C, LANES), BF16),
        qkl=pltpu.VMEM((2, C, TC), BF16),
        qkr=pltpu.VMEM((2, C, TC), BF16),
        kl=pltpu.VMEM((4, C, TC), BF16),
        kr=pltpu.VMEM((4, C, TC), BF16),
        gacc=pltpu.VMEM((C, 2 * TC), F32),
        sacc=pltpu.VMEM((C, 2 * TC), F32),
        wacc=pltpu.VMEM((4 * C, 4 * C), F32),
        rs_send=pltpu.VMEM((na, 2 * cr, TC), BF16),
        rs_recv=pltpu.VMEM((na, 2 * cr, TC), BF16),
        zb=pltpu.VMEM((nz, 2 * cr, TC), F32),
        ag=pltpu.VMEM((na, 2 * cr, TC), BF16),
        cacc=pltpu.VMEM((C, TC), F32),
        racc=pltpu.VMEM((C, TC), F32),
        cgs=pltpu.VMEM((nr, C // nr, TC), F32),
        cgr=pltpu.VMEM((nr, C // nr, TC), F32),
        rgs=pltpu.VMEM((nc, C // nc, TC), F32),
        rgr=pltpu.VMEM((nc, C // nc, TC), F32),
        feat_sems=pltpu.SemaphoreType.DMA((4,)),
        halo_send=pltpu.SemaphoreType.DMA((8,)),
        halo_recv=pltpu.SemaphoreType.DMA((8,)),
        grad_send=pltpu.SemaphoreType.DMA((8,)),
        grad_recv=pltpu.SemaphoreType.DMA((8,)),
        red_sems=pltpu.SemaphoreType.DMA((6,)),
        out_sems=pltpu.SemaphoreType.DMA((4,)),
    )
    outs = pl.pallas_call(
        functools.partial(kernel, nr, nc),
        out_shape=(
            jax.ShapeDtypeStruct((C, TR, TC), BF16),
            jax.ShapeDtypeStruct((C // nc, TR), F32),
            jax.ShapeDtypeStruct((C // nr, TC), F32),
            jax.ShapeDtypeStruct((9, C, C), F32),
            jax.ShapeDtypeStruct((C, C), F32),
            jax.ShapeDtypeStruct((1, C), F32),
            jax.ShapeDtypeStruct((1, C), F32),
        ),
        in_specs=[vmem] * 8,
        out_specs=(vmem,) * 7,
        scratch_shapes=list(scratch.values()),
        compiler_params=pltpu.CompilerParams(
            collective_id=0, has_side_effects=True, vmem_limit_bytes=48 * 1024 * 1024
        ),
    )(
        pair_in,
        row_feat,
        col_feat,
        cotangent,
        conv_weight,
        gain.reshape(1, C),
        shift.reshape(1, C),
        proj,
    )
    return (*outs[:5], outs[5].reshape(C), outs[6].reshape(C))


def solution(mesh):
    return jax.shard_map(
        functools.partial(shards, mesh.shape["row"], mesh.shape["col"]),
        mesh=mesh,
        in_specs=(
            P(None, "row", "col"),
            P("col", "row"),
            P("row", "col"),
            P(None, "row", "col"),
            P(),
            P(),
            P(),
            P(),
        ),
        out_specs=(P(None, "row", "col"), P("col", "row"), P("row", "col"), P(), P(), P(), P()),
        check_vma=False,
    )
```

```python
import functools
import math

import jax
import jax.numpy as jnp
from jax import lax
from jax.experimental import pallas as pl
from jax.experimental.pallas import tpu as pltpu
from jax.sharding import PartitionSpec as P

C = 64
D = 8
TR = 32
TC = 128
PR = TR + 2 * D
LANES = PR * TC
OWN = D * TC
TILE = TR * TC
F32 = jnp.float32
BF16 = jnp.bfloat16
VMEM_LIMIT = 60 * 1024 * 1024
MESH = pl.DeviceIdType.MESH


def dot(a, b):
    return lax.dot_general(a, b, (((1,), (0,)), ((), ())), preferred_element_type=F32)


def dot_nt(a, b):
    return lax.dot_general(a, b, (((1,), (1,)), ((), ())), preferred_element_type=F32)


def kernel(
    nr,
    nc,
    pair_in,
    rowf_in,
    colf_in,
    cot_in,
    w_in,
    gain_in,
    shift_in,
    proj_in,
    pg_out,
    rowg_out,
    colg_out,
    convg_out,
    projg_out,
    gaing_out,
    shiftg_out,
    pg_ref,
    rowg_ref,
    colg_ref,
    convg_ref,
    projg_ref,
    gaing_ref,
    shiftg_ref,
    pair_ref,
    rowf_ref,
    colf_ref,
    cot_ref,
    w_ref,
    gain_ref,
    shift_ref,
    proj_ref,
    xs,
    wf,
    pt,
    wd,
    gainb,
    shiftb,
    rf,
    cf,
    cfull,
    pc,
    rsend,
    csend,
    rnear,
    cnear,
    s2,
    gh,
    c2,
    pkl,
    pkr,
    hl,
    hr,
    gz,
    g2,
    qkl,
    qkr,
    kl,
    kr,
    wacc,
    rs_send,
    rs_recv,
    zb,
    ag,
    cacc,
    cgs,
    cgr,
    rgs,
    rgr,
    in_sems,
    store_sems,
    feat_sems,
    side_sems,
    halo_send,
    halo_recv,
    grad_send,
    grad_recv,
    red_sems,
    out_sems,
):
    row = lax.axis_index("row")
    col = lax.axis_index("col")
    nz = nr // 4
    na = 4 * nc
    cr = 256 // na
    cpr = C // nr
    cpc = C // nc
    zi = row // 4
    ai = lax.rem(row, 4) * nc + col
    up, down = lax.rem(row + nr - 1, nr), lax.rem(row + 1, nr)
    left, right = lax.rem(col + nc - 1, nc), lax.rem(col + 1, nc)
    bins = TR * nr

    def row_peer(k):
        return (lax.rem(row + k, nr), col)

    def col_peer(k):
        return (row, lax.rem(col + k, nc))

    def a_peer(k):
        idx = lax.rem(ai + k, na)
        return (zi * 4 + idx // nc, lax.rem(idx, nc))

    def z_peer(k):
        return (lax.rem(zi + k, nz) * 4 + lax.rem(row, 4), col)

    barrier = pltpu.get_barrier_semaphore()

    def greet(peer, count):
        def body(k, _):
            pl.semaphore_signal(barrier, inc=1, device_id=peer(k), device_id_type=MESH)
            return 0

        lax.fori_loop(1, count, body, 0)

    greet(row_peer, nr)
    greet(a_peer, na)
    for dr in (up, down):
        for dc in (left, right):
            pl.semaphore_signal(barrier, inc=1, device_id=(dr, dc), device_id_type=MESH)

    loads = [
        pltpu.make_async_copy(src, dst, in_sems.at[i])
        for i, (src, dst) in enumerate(
            (
                (rowf_in, rowf_ref),
                (colf_in, colf_ref),
                (pair_in, pair_ref),
                (cot_in, cot_ref),
                (w_in, w_ref),
                (proj_in, proj_ref),
                (gain_in, gain_ref),
                (shift_in, shift_ref),
            )
        )
    ]
    for load in loads:
        load.start()
    pending = []
    recvs = {}
    outputs = (
        (pg_ref, pg_out),
        (rowg_ref, rowg_out),
        (colg_ref, colg_out),
        (convg_ref, convg_out),
        (projg_ref, projg_out),
        (gaing_ref, gaing_out),
        (shiftg_ref, shiftg_out),
    )

    def store(first, last):
        for i in range(first, last):
            copy = pltpu.make_async_copy(*outputs[i], store_sems.at[i])
            copy.start()
            pending.append(copy.wait)


    lane = lax.broadcasted_iota(jnp.int32, (C, TC), 1)

    def packed(parts, edge):
        result = jnp.zeros((C, TC), F32)
        for k, x in enumerate(parts):
            shift = (8 * k + edge) % TC
            moved = pltpu.roll(x, shift, 1) if shift else x
            result = jnp.where(lane // 8 == k, moved, result)
        return result.astype(BF16)

    def halo_copies(center, base, target, lsend, rsend, lrecv, rrecv, ssem, rsem):
        plan = (
            (lsend.at[0], rrecv.at[3], (up, left)),
            (lsend.at[1], rrecv.at[0], (down, left)),
            (rsend.at[0], lrecv.at[3], (up, right)),
            (rsend.at[1], lrecv.at[0], (down, right)),
            (lsend, rrecv.at[pl.ds(1, 2)], (row, left)),
            (rsend, lrecv.at[pl.ds(1, 2)], (row, right)),
            (
                center.at[pl.ds(0, C), pl.ds(base, OWN)],
                target.at[pl.ds(0, C), pl.ds(OWN + TILE, OWN)],
                (up, col),
            ),
            (
                center.at[pl.ds(0, C), pl.ds(base + TILE - OWN, OWN)],
                target.at[pl.ds(0, C), pl.ds(0, OWN)],
                (down, col),
            ),
        )
        return [
            pltpu.make_async_remote_copy(src, dst, ssem.at[i], rsem.at[i], device, MESH)
            for i, (src, dst, device) in enumerate(plan)
        ]

    def clear_edges(lrecv, rrecv):
        @pl.when(row == 0)
        def _():
            lrecv[0] = jnp.zeros((C, TC), BF16)
            rrecv[0] = jnp.zeros((C, TC), BF16)

        @pl.when(row == nr - 1)
        def _():
            lrecv[3] = jnp.zeros((C, TC), BF16)
            rrecv[3] = jnp.zeros((C, TC), BF16)

        @pl.when(col == 0)
        def _():
            lrecv[...] = jnp.zeros_like(lrecv)

        @pl.when(col == nc - 1)
        def _():
            rrecv[...] = jnp.zeros_like(rrecv)

    def set_edges(ref, lrecv, rrecv):
        for b in range(4):
            lo = lrecv[b].astype(F32)
            hi = rrecv[b].astype(F32)
            for k in range(16):
                r = 16 * b + k - 8
                if not 0 <= r < PR:
                    continue
                from_left = pltpu.roll(lo, (TC - 8 * k) % TC, 1) if k else lo
                from_right = pltpu.roll(hi, 120 - 8 * k, 1) if k < 15 else hi
                at_left = ref.at[pl.ds(0, C), pl.ds(r * TC, TC)]
                at_right = ref.at[pl.ds(2 * C, C), pl.ds(r * TC, TC)]
                at_left[...] = jnp.where(
                    lane < 8, from_left, at_left[...].astype(F32)
                ).astype(BF16)
                at_right[...] = jnp.where(
                    lane >= 120, from_right, at_right[...].astype(F32)
                ).astype(BF16)

    for i in range(3):
        loads[i].wait()
    rf[col] = jnp.concatenate(
        [rowf_ref[...].astype(F32), jnp.zeros((cpc, TC - TR), F32)], axis=1
    )
    cf[row] = colf_ref[...].astype(F32)
    for i in range(8):
        xs[pl.ds(i * 256, 256), :] = pair_ref[pl.ds(i * 8, 8)].astype(F32).reshape(256, TC)
    for b in range(2):
        parts = []
        for k in range(16):
            r = 16 * b + k
            x = xs[pl.ds(r, C, stride=TR), :]
            pc[:, pl.ds(OWN + r * TC, TC)] = x.astype(BF16)
            parts.append(x)
        pkl[b] = packed(parts, 0)
        pkr[b] = packed(parts, 8)

    pl.semaphore_wait(barrier, (nr - 1) + (na - 1) + 4)

    def rf_copy(k):
        return pltpu.make_async_remote_copy(
            rf.at[col], rf.at[col], feat_sems.at[0], feat_sems.at[1], col_peer(k), MESH
        )

    def cf_copy(k):
        return pltpu.make_async_remote_copy(
            cf.at[row], cf.at[row], feat_sems.at[2], feat_sems.at[3], row_peer(k), MESH
        )

    def start_all(copy, count):
        def body(k, _):
            copy(k).start()
            return 0

        lax.fori_loop(1, count, body, 0)

    def wait_bytes(ref, sem):
        pltpu.make_async_copy(ref, ref, sem).wait()

    def wait_later(ref, send_sem, recv_sem, name):
        pending.append(lambda: wait_bytes(ref, send_sem))
        recvs[name] = lambda: wait_bytes(ref, recv_sem)

    def arrived(name):
        recvs.pop(name)()

    start_all(rf_copy, nc)
    start_all(cf_copy, nr)
    wait_later(rf.at[pl.ds(0, nc - 1)], feat_sems.at[0], feat_sems.at[1], "rf")
    wait_later(cf.at[pl.ds(0, nr - 1)], feat_sems.at[2], feat_sems.at[3], "cf")
    copies = halo_copies(pc, OWN, pc, pkl, pkr, hl, hr, halo_send, halo_recv)
    for i, copy in enumerate(copies):
        copy.start()
        pending.append(copy.wait_send)
        recvs[f"halo{i}"] = copy.wait_recv

    for i in range(3, 8):
        loads[i].wait()
    for i in range(8):
        xs[pl.ds(i * 256, 256), :] = cot_ref[pl.ds(i * 8, 8)].astype(F32).reshape(256, TC)
    for r in range(TR):
        c2[:, pl.ds(OWN + r * TC, TC)] = xs[pl.ds(r, C, stride=TR), :].astype(BF16)
    zeros = jnp.zeros((C, OWN), BF16)
    for part in (0, PR - D):
        c2[:, pl.ds(part * TC, OWN)] = zeros
        s2[pl.ds(3 * C, C), pl.ds(part * TC, OWN)] = zeros
    for part in (0, 1, 6, 7):
        gz[:, pl.ds(part * OWN, OWN)] = zeros
    for p in range(3):
        wf[p] = jnp.concatenate([w_ref[3 * p + q] for q in range(3)], axis=1)
        wd[p] = jnp.concatenate(
            [w_ref[3 * (2 - p) + 2 - q].astype(F32).T for q in range(3)], axis=1
        ).astype(BF16)
    pt[...] = proj_ref[...].astype(F32).T.astype(BF16)
    eye = lax.broadcasted_iota(jnp.int32, (C, C), 0) == lax.broadcasted_iota(jnp.int32, (C, C), 1)
    for src, dst in ((gain_ref, gainb), (shift_ref, shiftb)):
        column = jnp.sum(jnp.where(eye, src[...], 0.0), axis=1, keepdims=True)
        dst[...] = jnp.broadcast_to(column, (C, 2 * TC))
    arrived("rf")
    arrived("cf")

    for i in range(nr):
        cfull[pl.ds(i * cpr, cpr), :] = cf[i]
    row_full = rf[...].reshape(C, TC)
    col_full = cfull[...]
    rsend[...] = row_full.astype(BF16)
    csend[...] = col_full.astype(BF16)
    side_copies = [
        pltpu.make_async_remote_copy(
            src, dst, side_sems.at[2 * i], side_sems.at[2 * i + 1], device, MESH
        )
        for i, (src, dst, device) in enumerate(
            (
                (csend, cnear.at[1], (row, left)),
                (csend, cnear.at[0], (row, right)),
                (rsend, rnear.at[1], (up, col)),
                (rsend, rnear.at[0], (down, col)),
            )
        )
    ]
    for i, copy in enumerate(side_copies):
        copy.start()
        pending.append(copy.wait_send)
        recvs[f"side{i}"] = copy.wait_recv

    def activate(r, rows, at):
        pre = pc[:, pl.ds(r * TC, TC)].astype(F32) + rows[:, at : at + 1] + col_full
        return jnp.maximum(pre, 0.0)

    def place(ref, r, x):
        ref[pl.ds(0, C), pl.ds(r * TC, TC)] = pltpu.roll(x, 8, 1).astype(BF16)
        ref[pl.ds(C, C), pl.ds(r * TC, TC)] = x.astype(BF16)
        ref[pl.ds(2 * C, C), pl.ds(r * TC, TC)] = pltpu.roll(x, 120, 1).astype(BF16)

    for r in range(TR):
        place(s2, D + r, activate(D + r, row_full, r))
    for i in range(4):
        arrived(f"side{i}")
    for i in range(8):
        arrived(f"halo{i}")
    above, below = rnear[0].astype(F32), rnear[1].astype(F32)
    for r in range(D):
        top = activate(r, above, TR - D + r)
        place(s2, r, jnp.where(row > 0, top, 0.0))
        bottom = activate(D + TR + r, below, r)
        place(s2, D + TR + r, jnp.where(row < nr - 1, bottom, 0.0))

    def spread(first, divide):
        source = lax.broadcasted_iota(jnp.int32, (TC, TC), 0)
        target = lax.broadcasted_iota(jnp.int32, (TC, TC), 1)
        wanted = target // 8 if divide else target % 8
        return (source == first + wanted).astype(BF16)

    per_row = (
        dot(rnear[0], spread(TR - 16, True)),
        dot(rsend[...], spread(0, True)),
        dot(rsend[...], spread(16, True)),
        dot(rnear[1], spread(0, True)),
    )
    per_col = (dot(cnear[0], spread(TC - 8, False)), dot(cnear[1], spread(0, False)))
    for b in range(4):
        for buffer, feature in ((hl, per_col[0]), (hr, per_col[1])):
            pre = buffer[b].astype(F32) + per_row[b] + feature
            buffer[b] = jnp.maximum(pre, 0.0).astype(BF16)
    clear_edges(hl, hr)
    set_edges(s2, hl, hr)

    gain, shift = gainb[...], shiftb[...]
    gain_sum = jnp.zeros((C, TC), F32)
    shift_sum = jnp.zeros((C, TC), F32)
    for i in range(TR // 2):
        here = pl.ds(OWN + i * 256, 256)
        conv_out = sum(
            dot(wf[p], s2[pl.ds(0, 3 * C), pl.ds(p * OWN + i * 256, 256)]) for p in range(3)
        )
        back = dot(pt[...], c2[:, here])
        normed = gain * conv_out + shift
        sigma = jax.nn.sigmoid(normed)
        s2[pl.ds(3 * C, C), here] = (normed * sigma).astype(BF16)
        normed_grad = back * sigma * (1.0 + normed * (1.0 - sigma))
        product = normed_grad * conv_out
        gain_sum += product[:, :TC] + product[:, TC:]
        shift_sum += normed_grad[:, :TC] + normed_grad[:, TC:]
        gz[:, pl.ds(2 * OWN + i * 256, 256)] = (gain * normed_grad).astype(BF16)
    for b in range(2):
        parts = [
            gz[:, pl.ds(2 * OWN + (16 * b + k) * TC, TC)].astype(F32) for k in range(16)
        ]
        qkl[b] = packed(parts, 0)
        qkr[b] = packed(parts, 8)
    grad_copies = halo_copies(gz, 2 * OWN, gh, qkl, qkr, kl, kr, grad_send, grad_recv)
    for i, copy in enumerate(grad_copies):
        copy.start()
        pending.append(copy.wait_send)
        recvs[f"grad{i}"] = copy.wait_recv

    total = jnp.zeros((4 * C, 4 * C), F32)
    step = 1024
    for base in range(0, LANES, step):
        lhs = jnp.concatenate(
            [
                gz[:, pl.ds(base + 2 * OWN, step)],
                gz[:, pl.ds(base + OWN, step)],
                gz[:, pl.ds(base, step)],
                c2[:, pl.ds(base, step)],
            ],
            axis=0,
        )
        total += dot_nt(lhs, s2[:, pl.ds(base, step)])
    wacc[...] = total
    wacc[pl.ds(0, C), pl.ds(3 * C, 1)] = jnp.sum(gain_sum, axis=1, keepdims=True)
    wacc[pl.ds(0, C), pl.ds(3 * C + 1, 1)] = jnp.sum(shift_sum, axis=1, keepdims=True)

    for a in range(na):
        rs_send[a] = jnp.concatenate(
            [wacc[pl.ds(a * cr, cr), pl.ds(0, TC)], wacc[pl.ds(a * cr, cr), pl.ds(TC, TC)]], axis=0
        ).astype(BF16)

    def rs_copy(k):
        idx = lax.rem(ai + k, na)
        return pltpu.make_async_remote_copy(
            rs_send.at[idx], rs_recv.at[ai], red_sems.at[0], red_sems.at[1], a_peer(k), MESH
        )

    start_all(rs_copy, na)
    wait_later(rs_send.at[pl.ds(0, na - 1)], red_sems.at[0], red_sems.at[1], "rs")
    rs_recv[ai] = rs_send[ai]

    for r in range(TR):
        place(g2, D + r, gz[:, pl.ds(2 * OWN + r * TC, TC)].astype(F32))
    for i in range(8):
        arrived(f"grad{i}")
    for r in range(D):
        top = gh[:, pl.ds(r * TC, TC)].astype(F32)
        place(g2, r, jnp.where(row > 0, top, 0.0))
        bottom = gh[:, pl.ds(OWN + TILE + r * TC, TC)].astype(F32)
        place(g2, D + TR + r, jnp.where(row < nr - 1, bottom, 0.0))
    clear_edges(kl, kr)
    set_edges(g2, kl, kr)
    arrived("rs")
    zb[zi] = jnp.sum(rs_recv[...].astype(F32), axis=0)

    def z_copy(k):
        return pltpu.make_async_remote_copy(
            zb.at[zi], zb.at[zi], red_sems.at[2], red_sems.at[3], z_peer(k), MESH
        )

    start_all(z_copy, nz)
    wait_later(zb.at[pl.ds(0, nz - 1)], red_sems.at[2], red_sems.at[3], "z")
    root = math.sqrt(bins)
    col_sum = jnp.zeros((C, TC), F32)
    row_sum = jnp.zeros((C, TC), F32)
    for i in range(TR // 2):
        here = pl.ds(OWN + i * 256, 256)
        act_grad = sum(
            dot(wd[p], g2[:, pl.ds(p * OWN + i * 256, 256)]) for p in range(3)
        )
        active = s2[pl.ds(C, C), here].astype(F32)
        pre_grad = jnp.where(active > 0, act_grad, 0.0)
        col_sum += pre_grad[:, :TC] + pre_grad[:, TC:]
        pair_grad = pre_grad + c2[:, here].astype(F32)
        for half in range(2):
            r = 2 * i + half
            part = slice(half * TC, half * TC + TC)
            row_sum = jnp.where(
                lane == r, jnp.sum(pre_grad[:, part], axis=1, keepdims=True), row_sum
            )
            xs[pl.ds(r, C, stride=TR), :] = pair_grad[:, part]
    cacc[...] = col_sum
    for i in range(nr):
        cgs[i] = cacc[pl.ds(i * cpr, cpr), :]
    rgs[...] = row_sum.reshape(nc, cpc, TC)

    def cg_copy(k):
        idx = lax.rem(row + k, nr)
        return pltpu.make_async_remote_copy(
            cgs.at[idx], cgr.at[row], out_sems.at[0], out_sems.at[1], row_peer(k), MESH
        )

    def rg_copy(k):
        idx = lax.rem(col + k, nc)
        return pltpu.make_async_remote_copy(
            rgs.at[idx], rgr.at[col], out_sems.at[2], out_sems.at[3], col_peer(k), MESH
        )

    start_all(cg_copy, nr)
    start_all(rg_copy, nc)
    wait_later(cgs.at[pl.ds(0, nr - 1)], out_sems.at[0], out_sems.at[1], "cg")
    wait_later(rgs.at[pl.ds(0, nc - 1)], out_sems.at[2], out_sems.at[3], "rg")
    cgr[row] = cgs[row]
    rgr[col] = rgs[col]

    arrived("z")
    ag[ai] = (jnp.sum(zb[...], axis=0) * (1.0 / bins)).astype(BF16)

    def ag_copy(k):
        return pltpu.make_async_remote_copy(
            ag.at[ai], ag.at[ai], red_sems.at[4], red_sems.at[5], a_peer(k), MESH
        )

    start_all(ag_copy, na)
    wait_later(ag.at[pl.ds(0, na - 1)], red_sems.at[4], red_sems.at[5], "ag")

    for i in range(8):
        pg_ref[pl.ds(i * 8, 8)] = xs[pl.ds(i * 256, 256), :].reshape(8, TR, TC).astype(BF16)

    arrived("cg")
    arrived("rg")
    colg_ref[...] = jnp.sum(cgr[...], axis=0) * (1.0 / root)
    rowg_ref[...] = jnp.sum(rgr[...], axis=0)[:, :TR] * (1.0 / root)

    store(0, 1)
    arrived("ag")
    store(1, 3)
    total = ag[...].astype(F32)
    low = total[:, :cr].reshape(256, TC)
    high = total[:, cr:].reshape(256, TC)
    for p in range(3):
        convg_ref[3 * p] = low[C * p : C * p + C, :C]
        convg_ref[3 * p + 1] = low[C * p : C * p + C, C:]
        convg_ref[3 * p + 2] = high[C * p : C * p + C, :C]
    projg_ref[...] = high[3 * C :, C:]
    gaing_ref[...] = jnp.sum(jnp.where(eye, high[:C, C : C + 1], 0.0), axis=0, keepdims=True)
    shiftg_ref[...] = jnp.sum(jnp.where(eye, high[:C, C + 1 : C + 2], 0.0), axis=0, keepdims=True)

    store(3, 7)
    for wait in (*recvs.values(), *pending):
        wait()


def store_kernel(*refs):
    sources, targets, stages, sems = refs[:7], refs[7:14], refs[14:21], refs[21]
    loads = [
        pltpu.make_async_copy(a, b, sems.at[i]) for i, (a, b) in enumerate(zip(sources, stages))
    ]
    stores = [
        pltpu.make_async_copy(a, b, sems.at[i]) for i, (a, b) in enumerate(zip(stages, targets))
    ]
    for copy in loads:
        copy.start()
    for load, store in zip(loads, stores):
        load.wait()
        store.start()
    for copy in stores:
        copy.wait()


def shards(nr, nc, pair_in, row_feat, col_feat, cotangent, conv_weight, gain, shift, proj):
    na, nz = 4 * nc, nr // 4
    cr = 256 // na
    hbm = pl.BlockSpec(memory_space=pltpu.HBM)
    scratch = dict(
        pg_ref=pltpu.VMEM((C, TR, TC), BF16),
        rowg_ref=pltpu.VMEM((C // nc, TR), F32),
        colg_ref=pltpu.VMEM((C // nr, TC), F32),
        convg_ref=pltpu.VMEM((9, C, C), F32),
        projg_ref=pltpu.VMEM((C, C), F32),
        gaing_ref=pltpu.VMEM((1, C), F32),
        shiftg_ref=pltpu.VMEM((1, C), F32),
        pair_ref=pltpu.VMEM((C, TR, TC), BF16),
        rowf_ref=pltpu.VMEM((C // nc, TR), BF16),
        colf_ref=pltpu.VMEM((C // nr, TC), BF16),
        cot_ref=pltpu.VMEM((C, TR, TC), BF16),
        w_ref=pltpu.VMEM((9, C, C), BF16),
        gain_ref=pltpu.VMEM((1, C), F32),
        shift_ref=pltpu.VMEM((1, C), F32),
        proj_ref=pltpu.VMEM((C, C), BF16),
        xs=pltpu.VMEM((C * TR, TC), F32),
        wf=pltpu.VMEM((3, C, 3 * C), BF16),
        pt=pltpu.VMEM((C, C), BF16),
        wd=pltpu.VMEM((3, C, 3 * C), BF16),
        gainb=pltpu.VMEM((C, 2 * TC), F32),
        shiftb=pltpu.VMEM((C, 2 * TC), F32),
        rf=pltpu.VMEM((nc, C // nc, TC), F32),
        cf=pltpu.VMEM((nr, C // nr, TC), F32),
        cfull=pltpu.VMEM((C, TC), F32),
        pc=pltpu.VMEM((C, LANES), BF16),
        rsend=pltpu.VMEM((C, TC), BF16),
        csend=pltpu.VMEM((C, TC), BF16),
        rnear=pltpu.VMEM((2, C, TC), BF16),
        cnear=pltpu.VMEM((2, C, TC), BF16),
        s2=pltpu.VMEM((4 * C, LANES), BF16),
        gh=pltpu.VMEM((C, LANES), BF16),
        c2=pltpu.VMEM((C, LANES), BF16),
        pkl=pltpu.VMEM((2, C, TC), BF16),
        pkr=pltpu.VMEM((2, C, TC), BF16),
        hl=pltpu.VMEM((4, C, TC), BF16),
        hr=pltpu.VMEM((4, C, TC), BF16),
        gz=pltpu.VMEM((C, LANES + 2 * OWN), BF16),
        g2=pltpu.VMEM((3 * C, LANES), BF16),
        qkl=pltpu.VMEM((2, C, TC), BF16),
        qkr=pltpu.VMEM((2, C, TC), BF16),
        kl=pltpu.VMEM((4, C, TC), BF16),
        kr=pltpu.VMEM((4, C, TC), BF16),
        wacc=pltpu.VMEM((4 * C, 4 * C), F32),
        rs_send=pltpu.VMEM((na, 2 * cr, TC), BF16),
        rs_recv=pltpu.VMEM((na, 2 * cr, TC), BF16),
        zb=pltpu.VMEM((nz, 2 * cr, TC), F32),
        ag=pltpu.VMEM((na, 2 * cr, TC), BF16),
        cacc=pltpu.VMEM((C, TC), F32),
        cgs=pltpu.VMEM((nr, C // nr, TC), F32),
        cgr=pltpu.VMEM((nr, C // nr, TC), F32),
        rgs=pltpu.VMEM((nc, C // nc, TC), F32),
        rgr=pltpu.VMEM((nc, C // nc, TC), F32),
        in_sems=pltpu.SemaphoreType.DMA((8,)),
        store_sems=pltpu.SemaphoreType.DMA((7,)),
        feat_sems=pltpu.SemaphoreType.DMA((4,)),
        side_sems=pltpu.SemaphoreType.DMA((8,)),
        halo_send=pltpu.SemaphoreType.DMA((8,)),
        halo_recv=pltpu.SemaphoreType.DMA((8,)),
        grad_send=pltpu.SemaphoreType.DMA((8,)),
        grad_recv=pltpu.SemaphoreType.DMA((8,)),
        red_sems=pltpu.SemaphoreType.DMA((6,)),
        out_sems=pltpu.SemaphoreType.DMA((4,)),
    )
    shapes = (
        jax.ShapeDtypeStruct((C, TR, TC), BF16),
        jax.ShapeDtypeStruct((C // nc, TR), F32),
        jax.ShapeDtypeStruct((C // nr, TC), F32),
        jax.ShapeDtypeStruct((9, C, C), F32),
        jax.ShapeDtypeStruct((C, C), F32),
        jax.ShapeDtypeStruct((1, C), F32),
        jax.ShapeDtypeStruct((1, C), F32),
    )
    outs = pl.pallas_call(
        functools.partial(kernel, nr, nc),
        out_shape=shapes,
        in_specs=[hbm] * 8,
        out_specs=(hbm,) * 7,
        scratch_shapes=list(scratch.values()),
        compiler_params=pltpu.CompilerParams(
            collective_id=0, has_side_effects=True, vmem_limit_bytes=VMEM_LIMIT
        ),
    )(
        pair_in,
        row_feat,
        col_feat,
        cotangent,
        conv_weight,
        gain.reshape(1, C),
        shift.reshape(1, C),
        proj,
    )
    outs = pl.pallas_call(
        store_kernel,
        out_shape=shapes,
        in_specs=[hbm] * 7,
        out_specs=(hbm,) * 7,
        scratch_shapes=[
            *(pltpu.VMEM(shape.shape, shape.dtype) for shape in shapes),
            pltpu.SemaphoreType.DMA((7,)),
        ],
        compiler_params=pltpu.CompilerParams(vmem_limit_bytes=VMEM_LIMIT),
    )(*outs)
    return (*outs[:5], outs[5].reshape(C), outs[6].reshape(C))


def solution(mesh):
    return jax.shard_map(
        functools.partial(shards, mesh.shape["row"], mesh.shape["col"]),
        mesh=mesh,
        in_specs=(
            P(None, "row", "col"),
            P("col", "row"),
            P("row", "col"),
            P(None, "row", "col"),
            P(),
            P(),
            P(),
            P(),
        ),
        out_specs=(P(None, "row", "col"), P("col", "row"), P("row", "col"), P(), P(), P(), P()),
        check_vma=False,
    )
```

```python
import functools
import math

import jax
import jax.numpy as jnp
from jax import lax
from jax.experimental import pallas as pl
from jax.experimental.pallas import tpu as pltpu
from jax.sharding import PartitionSpec as P

C = 64
D = 8
TR = 32
TC = 128
PR = TR + 2 * D
LANES = PR * TC
OWN = D * TC
TILE = TR * TC
F32 = jnp.float32
BF16 = jnp.bfloat16
VMEM_LIMIT = 40 * 1024 * 1024
MESH = pl.DeviceIdType.MESH


def dot(a, b):
    return lax.dot_general(a, b, (((1,), (0,)), ((), ())), preferred_element_type=F32)


def dot_nt(a, b):
    return lax.dot_general(a, b, (((1,), (1,)), ((), ())), preferred_element_type=F32)


def kernel(
    nr,
    nc,
    pair_in,
    rowf_in,
    colf_in,
    cot_in,
    w_in,
    gain_in,
    shift_in,
    proj_in,
    pg_ref,
    rowg_ref,
    colg_ref,
    convg_ref,
    projg_ref,
    gaing_ref,
    shiftg_ref,
    pair_ref,
    rowf_ref,
    colf_ref,
    cot_ref,
    w_ref,
    gain_ref,
    shift_ref,
    proj_ref,
    xs,
    wf,
    pt,
    wd,
    gainb,
    shiftb,
    rf,
    cf,
    cfull,
    pc,
    rsend,
    csend,
    rnear,
    cnear,
    s2,
    gh,
    c2,
    pkl,
    pkr,
    hl,
    hr,
    gz,
    g2,
    qkl,
    qkr,
    kl,
    kr,
    wacc,
    rs_send,
    rs_recv,
    zb,
    ag,
    cacc,
    cgs,
    cgr,
    rgs,
    rgr,
    in_sems,
    feat_sems,
    side_sems,
    halo_send,
    halo_recv,
    grad_send,
    grad_recv,
    red_sems,
    out_sems,
):
    row = lax.axis_index("row")
    col = lax.axis_index("col")
    nz = nr // 4
    na = 4 * nc
    cr = 256 // na
    cpr = C // nr
    cpc = C // nc
    zi = row // 4
    ai = lax.rem(row, 4) * nc + col
    up, down = lax.rem(row + nr - 1, nr), lax.rem(row + 1, nr)
    left, right = lax.rem(col + nc - 1, nc), lax.rem(col + 1, nc)
    bins = TR * nr

    def row_peer(k):
        return (lax.rem(row + k, nr), col)

    def col_peer(k):
        return (row, lax.rem(col + k, nc))

    def a_peer(k):
        idx = lax.rem(ai + k, na)
        return (zi * 4 + idx // nc, lax.rem(idx, nc))

    def z_peer(k):
        return (lax.rem(zi + k, nz) * 4 + lax.rem(row, 4), col)

    def far_first(count, ring):
        return sorted(range(1, count), key=lambda k: -min(k % ring, ring - k % ring))

    barrier = pltpu.get_barrier_semaphore()

    def greet(peer, count, ring):
        for k in far_first(count, ring):
            pl.semaphore_signal(barrier, inc=1, device_id=peer(k), device_id_type=MESH)

    greet(row_peer, nr, nr)
    greet(a_peer, na, nc)
    for dr in (up, down):
        for dc in (left, right):
            pl.semaphore_signal(barrier, inc=1, device_id=(dr, dc), device_id_type=MESH)

    loads = [
        pltpu.make_async_copy(src, dst, in_sems.at[i])
        for i, (src, dst) in enumerate(
            (
                (rowf_in, rowf_ref),
                (colf_in, colf_ref),
                (pair_in, pair_ref),
                (cot_in, cot_ref),
                (w_in, w_ref),
                (proj_in, proj_ref),
                (gain_in, gain_ref),
                (shift_in, shift_ref),
            )
        )
    ]
    for load in loads:
        load.start()
    pending = []
    recvs = {}
    lane = lax.broadcasted_iota(jnp.int32, (C, TC), 1)

    def packed(parts, edge):
        result = jnp.zeros((C, TC), BF16)
        for k, x in enumerate(parts):
            shift = (8 * k + edge) % TC
            moved = pltpu.roll(x, shift, 1) if shift else x
            result = jnp.where(lane // 8 == k, moved, result)
        return result

    def halo_copies(center, base, target, lsend, rsend, lrecv, rrecv, ssem, rsem):
        plan = (
            (lsend.at[0], rrecv.at[3], (up, left)),
            (lsend.at[1], rrecv.at[0], (down, left)),
            (rsend.at[0], lrecv.at[3], (up, right)),
            (rsend.at[1], lrecv.at[0], (down, right)),
            (lsend, rrecv.at[pl.ds(1, 2)], (row, left)),
            (rsend, lrecv.at[pl.ds(1, 2)], (row, right)),
            (
                center.at[pl.ds(0, C), pl.ds(base, OWN)],
                target.at[pl.ds(0, C), pl.ds(OWN + TILE, OWN)],
                (up, col),
            ),
            (
                center.at[pl.ds(0, C), pl.ds(base + TILE - OWN, OWN)],
                target.at[pl.ds(0, C), pl.ds(0, OWN)],
                (down, col),
            ),
        )
        return [
            pltpu.make_async_remote_copy(src, dst, ssem.at[i], rsem.at[i], device, MESH)
            for i, (src, dst, device) in enumerate(plan)
        ]

    def clear_edges(lrecv, rrecv):
        @pl.when(row == 0)
        def _():
            lrecv[0] = jnp.zeros((C, TC), BF16)
            rrecv[0] = jnp.zeros((C, TC), BF16)

        @pl.when(row == nr - 1)
        def _():
            lrecv[3] = jnp.zeros((C, TC), BF16)
            rrecv[3] = jnp.zeros((C, TC), BF16)

        @pl.when(col == 0)
        def _():
            lrecv[...] = jnp.zeros_like(lrecv)

        @pl.when(col == nc - 1)
        def _():
            rrecv[...] = jnp.zeros_like(rrecv)

    def set_edges(ref, lrecv, rrecv):
        for b in range(4):
            lo, hi = lrecv[b], rrecv[b]
            for k in range(16):
                r = 16 * b + k - 8
                if not 0 <= r < PR:
                    continue
                from_left = pltpu.roll(lo, (TC - 8 * k) % TC, 1) if k else lo
                from_right = pltpu.roll(hi, 120 - 8 * k, 1) if k < 15 else hi
                at_left = ref.at[pl.ds(0, C), pl.ds(r * TC, TC)]
                at_right = ref.at[pl.ds(2 * C, C), pl.ds(r * TC, TC)]
                at_left[...] = jnp.where(lane < 8, from_left, at_left[...])
                at_right[...] = jnp.where(lane >= 120, from_right, at_right[...])

    for i in range(3):
        loads[i].wait()
    rf[col] = jnp.concatenate(
        [rowf_ref[...].astype(F32), jnp.zeros((cpc, TC - TR), F32)], axis=1
    )
    cf[row] = colf_ref[...].astype(F32)
    for i in range(8):
        xs[pl.ds(i * 256, 256), :] = pair_ref[pl.ds(i * 8, 8)].astype(F32).reshape(256, TC)
    for b in range(2):
        parts = []
        for k in range(16):
            r = 16 * b + k
            x = xs[pl.ds(r, C, stride=TR), :].astype(BF16)
            pc[:, pl.ds(OWN + r * TC, TC)] = x
            parts.append(x)
        pkl[b] = packed(parts, 0)
        pkr[b] = packed(parts, 8)

    pl.semaphore_wait(barrier, (nr - 1) + (na - 1) + 4)

    def rf_copy(k):
        return pltpu.make_async_remote_copy(
            rf.at[col], rf.at[col], feat_sems.at[0], feat_sems.at[1], col_peer(k), MESH
        )

    def cf_copy(k):
        return pltpu.make_async_remote_copy(
            cf.at[row], cf.at[row], feat_sems.at[2], feat_sems.at[3], row_peer(k), MESH
        )

    def start_all(copy, count, ring):
        for k in far_first(count, ring):
            copy(k).start()

    def wait_bytes(ref, sem):
        pltpu.make_async_copy(ref, ref, sem).wait()

    def wait_later(ref, send_sem, recv_sem, name):
        pending.append(lambda: wait_bytes(ref, send_sem))
        recvs[name] = lambda: wait_bytes(ref, recv_sem)

    def arrived(name):
        recvs.pop(name)()

    start_all(cf_copy, nr, nr)
    start_all(rf_copy, nc, nc)
    wait_later(rf.at[pl.ds(0, nc - 1)], feat_sems.at[0], feat_sems.at[1], "rf")
    wait_later(cf.at[pl.ds(0, nr - 1)], feat_sems.at[2], feat_sems.at[3], "cf")
    copies = halo_copies(pc, OWN, pc, pkl, pkr, hl, hr, halo_send, halo_recv)
    for i, copy in enumerate(copies):
        copy.start()
        pending.append(copy.wait_send)
        recvs[f"halo{i}"] = copy.wait_recv

    for i in range(3, 8):
        loads[i].wait()
    for i in range(8):
        xs[pl.ds(i * 256, 256), :] = cot_ref[pl.ds(i * 8, 8)].astype(F32).reshape(256, TC)
    for r in range(TR):
        c2[:, pl.ds(OWN + r * TC, TC)] = xs[pl.ds(r, C, stride=TR), :].astype(BF16)
    zeros = jnp.zeros((C, OWN), BF16)
    for part in (0, PR - D):
        c2[:, pl.ds(part * TC, OWN)] = zeros
        s2[pl.ds(3 * C, C), pl.ds(part * TC, OWN)] = zeros
    for part in (0, 1, 6, 7):
        gz[:, pl.ds(part * OWN, OWN)] = zeros
    for p in range(3):
        wf[p] = jnp.concatenate([w_ref[3 * p + q] for q in range(3)], axis=1)
        wd[p] = jnp.concatenate(
            [w_ref[3 * (2 - p) + 2 - q].astype(F32).T for q in range(3)], axis=1
        ).astype(BF16)
    pt[...] = proj_ref[...].astype(F32).T.astype(BF16)
    eye = lax.broadcasted_iota(jnp.int32, (C, C), 0) == lax.broadcasted_iota(jnp.int32, (C, C), 1)
    for src, dst in ((gain_ref, gainb), (shift_ref, shiftb)):
        column = jnp.sum(jnp.where(eye, src[...], 0.0), axis=1, keepdims=True)
        dst[...] = jnp.broadcast_to(column, (C, 2 * TC))
    arrived("rf")
    arrived("cf")

    for i in range(nr):
        cfull[pl.ds(i * cpr, cpr), :] = cf[i]
    row_full = rf[...].reshape(C, TC)
    col_full = cfull[...]
    rsend[...] = row_full.astype(BF16)
    csend[...] = col_full.astype(BF16)
    side_copies = [
        pltpu.make_async_remote_copy(
            src, dst, side_sems.at[2 * i], side_sems.at[2 * i + 1], device, MESH
        )
        for i, (src, dst, device) in enumerate(
            (
                (csend, cnear.at[1], (row, left)),
                (csend, cnear.at[0], (row, right)),
                (rsend, rnear.at[1], (up, col)),
                (rsend, rnear.at[0], (down, col)),
            )
        )
    ]
    for i, copy in enumerate(side_copies):
        copy.start()
        pending.append(copy.wait_send)
        recvs[f"side{i}"] = copy.wait_recv

    def activate(r, rows, at):
        pre = pc[:, pl.ds(r * TC, TC)].astype(F32) + rows[:, at : at + 1] + col_full
        return jnp.maximum(pre, 0.0).astype(BF16)

    def place(ref, r, x):
        ref[pl.ds(0, C), pl.ds(r * TC, TC)] = pltpu.roll(x, 8, 1)
        ref[pl.ds(C, C), pl.ds(r * TC, TC)] = x
        ref[pl.ds(2 * C, C), pl.ds(r * TC, TC)] = pltpu.roll(x, 120, 1)

    for r in range(TR):
        place(s2, D + r, activate(D + r, row_full, r))
    for i in range(4):
        arrived(f"side{i}")
    for i in range(8):
        arrived(f"halo{i}")
    above, below = rnear[0].astype(F32), rnear[1].astype(F32)
    for r in range(D):
        top = activate(r, above, TR - D + r)
        place(s2, r, jnp.where(row > 0, top, jnp.zeros_like(top)))
        bottom = activate(D + TR + r, below, r)
        place(s2, D + TR + r, jnp.where(row < nr - 1, bottom, jnp.zeros_like(bottom)))

    def spread(first, divide):
        source = lax.broadcasted_iota(jnp.int32, (TC, TC), 0)
        target = lax.broadcasted_iota(jnp.int32, (TC, TC), 1)
        wanted = target // 8 if divide else target % 8
        return (source == first + wanted).astype(BF16)

    per_row = (
        dot(rnear[0], spread(TR - 16, True)),
        dot(rsend[...], spread(0, True)),
        dot(rsend[...], spread(16, True)),
        dot(rnear[1], spread(0, True)),
    )
    per_col = (dot(cnear[0], spread(TC - 8, False)), dot(cnear[1], spread(0, False)))
    for b in range(4):
        for buffer, feature in ((hl, per_col[0]), (hr, per_col[1])):
            pre = buffer[b].astype(F32) + per_row[b] + feature
            buffer[b] = jnp.maximum(pre, 0.0).astype(BF16)
    clear_edges(hl, hr)
    set_edges(s2, hl, hr)

    gain, shift = gainb[...], shiftb[...]
    gain_sum = jnp.zeros((C, TC), F32)
    shift_sum = jnp.zeros((C, TC), F32)
    for i in range(TR // 2):
        here = pl.ds(OWN + i * 256, 256)
        conv_out = sum(
            dot(wf[p], s2[pl.ds(0, 3 * C), pl.ds(p * OWN + i * 256, 256)]) for p in range(3)
        )
        back = dot(pt[...], c2[:, here])
        normed = gain * conv_out + shift
        sigma = jax.nn.sigmoid(normed)
        s2[pl.ds(3 * C, C), here] = (normed * sigma).astype(BF16)
        normed_grad = back * sigma * (1.0 + normed * (1.0 - sigma))
        product = normed_grad * conv_out
        gain_sum += product[:, :TC] + product[:, TC:]
        shift_sum += normed_grad[:, :TC] + normed_grad[:, TC:]
        gz[:, pl.ds(2 * OWN + i * 256, 256)] = (gain * normed_grad).astype(BF16)
    for b in range(2):
        parts = [
            gz[:, pl.ds(2 * OWN + (16 * b + k) * TC, TC)] for k in range(16)
        ]
        qkl[b] = packed(parts, 0)
        qkr[b] = packed(parts, 8)
    total = jnp.zeros((4 * C, 4 * C), F32)
    step = 1024
    for base in range(0, LANES, step):
        lhs = jnp.concatenate(
            [
                gz[:, pl.ds(base + 2 * OWN, step)],
                gz[:, pl.ds(base + OWN, step)],
                gz[:, pl.ds(base, step)],
                c2[:, pl.ds(base, step)],
            ],
            axis=0,
        )
        total += dot_nt(lhs, s2[:, pl.ds(base, step)])
    wacc[...] = total
    wacc[pl.ds(0, C), pl.ds(3 * C, 1)] = jnp.sum(gain_sum, axis=1, keepdims=True)
    wacc[pl.ds(0, C), pl.ds(3 * C + 1, 1)] = jnp.sum(shift_sum, axis=1, keepdims=True)

    for a in range(na):
        rs_send[a] = jnp.concatenate(
            [wacc[pl.ds(a * cr, cr), pl.ds(0, TC)], wacc[pl.ds(a * cr, cr), pl.ds(TC, TC)]], axis=0
        ).astype(BF16)

    def rs_copy(k):
        idx = lax.rem(ai + k, na)
        return pltpu.make_async_remote_copy(
            rs_send.at[idx], rs_recv.at[ai], red_sems.at[0], red_sems.at[1], a_peer(k), MESH
        )

    start_all(rs_copy, na, nc)
    wait_later(rs_send.at[pl.ds(0, na - 1)], red_sems.at[0], red_sems.at[1], "rs")
    rs_recv[ai] = rs_send[ai]

    grad_copies = halo_copies(gz, 2 * OWN, gh, qkl, qkr, kl, kr, grad_send, grad_recv)
    for i, copy in enumerate(grad_copies):
        copy.start()
        pending.append(copy.wait_send)
        recvs[f"grad{i}"] = copy.wait_recv

    for r in range(TR):
        place(g2, D + r, gz[:, pl.ds(2 * OWN + r * TC, TC)])
    arrived("rs")
    zb[zi] = jnp.sum(rs_recv[...].astype(F32), axis=0)

    def z_copy(k):
        return pltpu.make_async_remote_copy(
            zb.at[zi], zb.at[zi], red_sems.at[2], red_sems.at[3], z_peer(k), MESH
        )

    start_all(z_copy, nz, nz)
    wait_later(zb.at[pl.ds(0, nz - 1)], red_sems.at[2], red_sems.at[3], "z")
    for i in range(8):
        arrived(f"grad{i}")
    for r in range(D):
        top = gh[:, pl.ds(r * TC, TC)]
        place(g2, r, jnp.where(row > 0, top, jnp.zeros_like(top)))
        bottom = gh[:, pl.ds(OWN + TILE + r * TC, TC)]
        place(g2, D + TR + r, jnp.where(row < nr - 1, bottom, jnp.zeros_like(bottom)))
    clear_edges(kl, kr)
    set_edges(g2, kl, kr)
    root = math.sqrt(bins)
    col_sum = jnp.zeros((C, TC), F32)
    row_sum = jnp.zeros((C, TC), F32)
    for i in range(TR // 2):
        here = pl.ds(OWN + i * 256, 256)
        act_grad = sum(
            dot(wd[p], g2[:, pl.ds(p * OWN + i * 256, 256)]) for p in range(3)
        )
        active = s2[pl.ds(C, C), here].astype(F32)
        pre_grad = jnp.where(active > 0, act_grad, 0.0)
        col_sum += pre_grad[:, :TC] + pre_grad[:, TC:]
        pair_grad = pre_grad + c2[:, here].astype(F32)
        for half in range(2):
            r = 2 * i + half
            part = slice(half * TC, half * TC + TC)
            row_sum = jnp.where(
                lane == r, jnp.sum(pre_grad[:, part], axis=1, keepdims=True), row_sum
            )
            xs[pl.ds(r, C, stride=TR), :] = pair_grad[:, part]
    cacc[...] = col_sum
    for i in range(nr):
        cgs[i] = cacc[pl.ds(i * cpr, cpr), :]
    rgs[...] = row_sum.reshape(nc, cpc, TC)

    def cg_copy(k):
        idx = lax.rem(row + k, nr)
        return pltpu.make_async_remote_copy(
            cgs.at[idx], cgr.at[row], out_sems.at[0], out_sems.at[1], row_peer(k), MESH
        )

    def rg_copy(k):
        idx = lax.rem(col + k, nc)
        return pltpu.make_async_remote_copy(
            rgs.at[idx], rgr.at[col], out_sems.at[2], out_sems.at[3], col_peer(k), MESH
        )

    start_all(cg_copy, nr, nr)
    start_all(rg_copy, nc, nc)
    wait_later(cgs.at[pl.ds(0, nr - 1)], out_sems.at[0], out_sems.at[1], "cg")
    wait_later(rgs.at[pl.ds(0, nc - 1)], out_sems.at[2], out_sems.at[3], "rg")
    cgr[row] = cgs[row]
    rgr[col] = rgs[col]

    arrived("z")
    ag[ai] = (jnp.sum(zb[...], axis=0) * (1.0 / bins)).astype(BF16)

    def ag_copy(k):
        return pltpu.make_async_remote_copy(
            ag.at[ai], ag.at[ai], red_sems.at[4], red_sems.at[5], a_peer(k), MESH
        )

    start_all(ag_copy, na, nc)
    wait_later(ag.at[pl.ds(0, na - 1)], red_sems.at[4], red_sems.at[5], "ag")

    for i in range(8):
        pg_ref[pl.ds(i * 8, 8)] = xs[pl.ds(i * 256, 256), :].reshape(8, TR, TC).astype(BF16)

    arrived("cg")
    arrived("rg")
    colg_ref[...] = jnp.sum(cgr[...], axis=0) * (1.0 / root)
    rowg_ref[...] = jnp.sum(rgr[...], axis=0)[:, :TR] * (1.0 / root)

    arrived("ag")
    total = ag[...].astype(F32)
    low = total[:, :cr].reshape(256, TC)
    high = total[:, cr:].reshape(256, TC)
    for p in range(3):
        convg_ref[3 * p] = low[C * p : C * p + C, :C]
        convg_ref[3 * p + 1] = low[C * p : C * p + C, C:]
        convg_ref[3 * p + 2] = high[C * p : C * p + C, :C]
    projg_ref[...] = high[3 * C :, C:]
    gaing_ref[...] = jnp.sum(jnp.where(eye, high[:C, C : C + 1], 0.0), axis=0, keepdims=True)
    shiftg_ref[...] = jnp.sum(jnp.where(eye, high[:C, C + 1 : C + 2], 0.0), axis=0, keepdims=True)

    for wait in (*recvs.values(), *pending):
        wait()


def store_kernel(*refs):
    copies = [
        pltpu.make_async_copy(refs[i], refs[7 + i], refs[14].at[i]) for i in range(7)
    ]
    for copy in copies:
        copy.start()
    for copy in copies:
        copy.wait()


def shards(nr, nc, pair_in, row_feat, col_feat, cotangent, conv_weight, gain, shift, proj):
    na, nz = 4 * nc, nr // 4
    cr = 256 // na
    hbm = pl.BlockSpec(memory_space=pltpu.HBM)
    vmem = pl.BlockSpec(memory_space=pltpu.VMEM)
    scratch = dict(
        pair_ref=pltpu.VMEM((C, TR, TC), BF16),
        rowf_ref=pltpu.VMEM((C // nc, TR), BF16),
        colf_ref=pltpu.VMEM((C // nr, TC), BF16),
        cot_ref=pltpu.VMEM((C, TR, TC), BF16),
        w_ref=pltpu.VMEM((9, C, C), BF16),
        gain_ref=pltpu.VMEM((1, C), F32),
        shift_ref=pltpu.VMEM((1, C), F32),
        proj_ref=pltpu.VMEM((C, C), BF16),
        xs=pltpu.VMEM((C * TR, TC), F32),
        wf=pltpu.VMEM((3, C, 3 * C), BF16),
        pt=pltpu.VMEM((C, C), BF16),
        wd=pltpu.VMEM((3, C, 3 * C), BF16),
        gainb=pltpu.VMEM((C, 2 * TC), F32),
        shiftb=pltpu.VMEM((C, 2 * TC), F32),
        rf=pltpu.VMEM((nc, C // nc, TC), F32),
        cf=pltpu.VMEM((nr, C // nr, TC), F32),
        cfull=pltpu.VMEM((C, TC), F32),
        pc=pltpu.VMEM((C, LANES), BF16),
        rsend=pltpu.VMEM((C, TC), BF16),
        csend=pltpu.VMEM((C, TC), BF16),
        rnear=pltpu.VMEM((2, C, TC), BF16),
        cnear=pltpu.VMEM((2, C, TC), BF16),
        s2=pltpu.VMEM((4 * C, LANES), BF16),
        gh=pltpu.VMEM((C, LANES), BF16),
        c2=pltpu.VMEM((C, LANES), BF16),
        pkl=pltpu.VMEM((2, C, TC), BF16),
        pkr=pltpu.VMEM((2, C, TC), BF16),
        hl=pltpu.VMEM((4, C, TC), BF16),
        hr=pltpu.VMEM((4, C, TC), BF16),
        gz=pltpu.VMEM((C, LANES + 2 * OWN), BF16),
        g2=pltpu.VMEM((3 * C, LANES), BF16),
        qkl=pltpu.VMEM((2, C, TC), BF16),
        qkr=pltpu.VMEM((2, C, TC), BF16),
        kl=pltpu.VMEM((4, C, TC), BF16),
        kr=pltpu.VMEM((4, C, TC), BF16),
        wacc=pltpu.VMEM((4 * C, 4 * C), F32),
        rs_send=pltpu.VMEM((na, 2 * cr, TC), BF16),
        rs_recv=pltpu.VMEM((na, 2 * cr, TC), BF16),
        zb=pltpu.VMEM((nz, 2 * cr, TC), F32),
        ag=pltpu.VMEM((na, 2 * cr, TC), BF16),
        cacc=pltpu.VMEM((C, TC), F32),
        cgs=pltpu.VMEM((nr, C // nr, TC), F32),
        cgr=pltpu.VMEM((nr, C // nr, TC), F32),
        rgs=pltpu.VMEM((nc, C // nc, TC), F32),
        rgr=pltpu.VMEM((nc, C // nc, TC), F32),
        in_sems=pltpu.SemaphoreType.DMA((8,)),
        feat_sems=pltpu.SemaphoreType.DMA((4,)),
        side_sems=pltpu.SemaphoreType.DMA((8,)),
        halo_send=pltpu.SemaphoreType.DMA((8,)),
        halo_recv=pltpu.SemaphoreType.DMA((8,)),
        grad_send=pltpu.SemaphoreType.DMA((8,)),
        grad_recv=pltpu.SemaphoreType.DMA((8,)),
        red_sems=pltpu.SemaphoreType.DMA((6,)),
        out_sems=pltpu.SemaphoreType.DMA((4,)),
    )
    shapes = (
        jax.ShapeDtypeStruct((C, TR, TC), BF16),
        jax.ShapeDtypeStruct((C // nc, TR), F32),
        jax.ShapeDtypeStruct((C // nr, TC), F32),
        jax.ShapeDtypeStruct((9, C, C), F32),
        jax.ShapeDtypeStruct((C, C), F32),
        jax.ShapeDtypeStruct((1, C), F32),
        jax.ShapeDtypeStruct((1, C), F32),
    )
    outs = pl.pallas_call(
        functools.partial(kernel, nr, nc),
        out_shape=tuple(pltpu.VMEM(shape.shape, shape.dtype) for shape in shapes),
        in_specs=[hbm] * 8,
        out_specs=(vmem,) * 7,
        scratch_shapes=list(scratch.values()),
        compiler_params=pltpu.CompilerParams(
            collective_id=0, has_side_effects=True, vmem_limit_bytes=VMEM_LIMIT
        ),
    )(
        *(
            pltpu.with_memory_space_constraint(operand, pltpu.HBM)
            for operand in (
                pair_in,
                row_feat,
                col_feat,
                cotangent,
                conv_weight,
                gain.reshape(1, C),
                shift.reshape(1, C),
                proj,
            )
        )
    )
    outs = pl.pallas_call(
        store_kernel,
        out_shape=shapes,
        in_specs=[vmem] * 7,
        out_specs=(hbm,) * 7,
        scratch_shapes=[pltpu.SemaphoreType.DMA((7,))],
        compiler_params=pltpu.CompilerParams(vmem_limit_bytes=8 * 1024 * 1024),
    )(*outs)
    return (*outs[:5], outs[5].reshape(C), outs[6].reshape(C))


def solution(mesh):
    return jax.shard_map(
        functools.partial(shards, mesh.shape["row"], mesh.shape["col"]),
        mesh=mesh,
        in_specs=(
            P(None, "row", "col"),
            P("col", "row"),
            P("row", "col"),
            P(None, "row", "col"),
            P(),
            P(),
            P(),
            P(),
        ),
        out_specs=(P(None, "row", "col"), P("col", "row"), P("row", "col"), P(), P(), P(), P()),
        check_vma=False,
    )
```

```python
import functools
import math

import jax
import jax.numpy as jnp
from jax import lax
from jax.experimental import pallas as pl
from jax.experimental.pallas import tpu as pltpu
from jax.sharding import PartitionSpec as P

C = 64
D = 8
TR = 32
TC = 128
PR = TR + 2 * D
LANES = PR * TC
OWN = D * TC
TILE = TR * TC
F32 = jnp.float32
BF16 = jnp.bfloat16
VMEM_LIMIT = 40 * 1024 * 1024
MESH = pl.DeviceIdType.MESH


def dot(a, b):
    return lax.dot_general(a, b, (((1,), (0,)), ((), ())), preferred_element_type=F32)


def dot_nt(a, b):
    return lax.dot_general(a, b, (((1,), (1,)), ((), ())), preferred_element_type=F32)


def kernel(
    nr,
    nc,
    pair_in,
    rowf_in,
    colf_in,
    cot_in,
    w_in,
    gain_in,
    shift_in,
    proj_in,
    pg_ref,
    rowg_ref,
    colg_ref,
    convg_ref,
    projg_ref,
    gaing_ref,
    shiftg_ref,
    pair_ref,
    rowf_ref,
    colf_ref,
    cot_ref,
    w_ref,
    gain_ref,
    shift_ref,
    proj_ref,
    xs,
    wf,
    pt,
    wd,
    gainb,
    shiftb,
    rf,
    cf,
    cfull,
    pc,
    rsend,
    csend,
    rnear,
    cnear,
    s2,
    gh,
    c2,
    pkl,
    pkr,
    hl,
    hr,
    gz,
    g2,
    qkl,
    qkr,
    kl,
    kr,
    wacc,
    rs_send,
    rs_recv,
    zb,
    ag,
    cacc,
    cgs,
    cgr,
    rgs,
    rgr,
    in_sems,
    feat_sems,
    side_sems,
    halo_send,
    halo_recv,
    grad_send,
    grad_recv,
    red_sems,
    out_sems,
):
    row = lax.axis_index("row")
    col = lax.axis_index("col")
    nz = nr // 4
    na = 4 * nc
    cr = 256 // na
    cpr = C // nr
    cpc = C // nc
    zi = row // 4
    ai = lax.rem(row, 4) * nc + col
    up, down = lax.rem(row + nr - 1, nr), lax.rem(row + 1, nr)
    left, right = lax.rem(col + nc - 1, nc), lax.rem(col + 1, nc)
    bins = TR * nr

    def row_peer(k):
        return (lax.rem(row + k, nr), col)

    def col_peer(k):
        return (row, lax.rem(col + k, nc))

    def a_peer(k):
        idx = lax.rem(ai + k, na)
        return (zi * 4 + idx // nc, lax.rem(idx, nc))

    def z_peer(k):
        return (lax.rem(zi + k, nz) * 4 + lax.rem(row, 4), col)

    def far_first(count, ring):
        return sorted(range(1, count), key=lambda k: -min(k % ring, ring - k % ring))

    barrier = pltpu.get_barrier_semaphore()

    def greet(peer, count, ring):
        for k in far_first(count, ring):
            pl.semaphore_signal(barrier, inc=1, device_id=peer(k), device_id_type=MESH)

    for dr in (up, down):
        for dc in (left, right):
            pl.semaphore_signal(barrier, inc=1, device_id=(dr, dc), device_id_type=MESH)
    greet(row_peer, nr, nr)
    greet(a_peer, na, nc)
    loads = [
        pltpu.make_async_copy(src, dst, in_sems.at[i])
        for i, (src, dst) in enumerate(
            (
                (rowf_in, rowf_ref),
                (colf_in, colf_ref),
                (pair_in, pair_ref),
                (cot_in, cot_ref),
                (w_in, w_ref),
                (proj_in, proj_ref),
                (gain_in, gain_ref),
                (shift_in, shift_ref),
            )
        )
    ]
    for load in loads:
        load.start()
    pending = []
    recvs = {}
    lane = lax.broadcasted_iota(jnp.int32, (C, TC), 1)

    def packed(parts, edge):
        result = jnp.zeros((C, TC), BF16)
        for k, x in enumerate(parts):
            shift = (8 * k + edge) % TC
            moved = pltpu.roll(x, shift, 1) if shift else x
            result = jnp.where(lane // 8 == k, moved, result)
        return result

    def halo_copies(center, base, target, lsend, rsend, lrecv, rrecv, ssem, rsem):
        plan = (
            (lsend.at[0], rrecv.at[3], (up, left)),
            (lsend.at[1], rrecv.at[0], (down, left)),
            (rsend.at[0], lrecv.at[3], (up, right)),
            (rsend.at[1], lrecv.at[0], (down, right)),
            (lsend, rrecv.at[pl.ds(1, 2)], (row, left)),
            (rsend, lrecv.at[pl.ds(1, 2)], (row, right)),
            (
                center.at[pl.ds(0, C), pl.ds(base, OWN)],
                target.at[pl.ds(0, C), pl.ds(OWN + TILE, OWN)],
                (up, col),
            ),
            (
                center.at[pl.ds(0, C), pl.ds(base + TILE - OWN, OWN)],
                target.at[pl.ds(0, C), pl.ds(0, OWN)],
                (down, col),
            ),
        )
        return [
            pltpu.make_async_remote_copy(src, dst, ssem.at[i], rsem.at[i], device, MESH)
            for i, (src, dst, device) in enumerate(plan)
        ]

    def clear_edges(lrecv, rrecv):
        @pl.when(row == 0)
        def _():
            lrecv[0] = jnp.zeros((C, TC), BF16)
            rrecv[0] = jnp.zeros((C, TC), BF16)

        @pl.when(row == nr - 1)
        def _():
            lrecv[3] = jnp.zeros((C, TC), BF16)
            rrecv[3] = jnp.zeros((C, TC), BF16)

        @pl.when(col == 0)
        def _():
            lrecv[...] = jnp.zeros_like(lrecv)

        @pl.when(col == nc - 1)
        def _():
            rrecv[...] = jnp.zeros_like(rrecv)

    def set_edges(ref, lrecv, rrecv):
        for b in range(4):
            lo, hi = lrecv[b], rrecv[b]
            for k in range(16):
                r = 16 * b + k - 8
                if not 0 <= r < PR:
                    continue
                from_left = pltpu.roll(lo, (TC - 8 * k) % TC, 1) if k else lo
                from_right = pltpu.roll(hi, 120 - 8 * k, 1) if k < 15 else hi
                at_left = ref.at[pl.ds(0, C), pl.ds(r * TC, TC)]
                at_right = ref.at[pl.ds(2 * C, C), pl.ds(r * TC, TC)]
                at_left[...] = jnp.where(lane < 8, from_left, at_left[...])
                at_right[...] = jnp.where(lane >= 120, from_right, at_right[...])

    for i in range(3):
        loads[i].wait()
    rf[col] = jnp.concatenate(
        [rowf_ref[...].astype(F32), jnp.zeros((cpc, TC - TR), F32)], axis=1
    )
    cf[row] = colf_ref[...].astype(F32)
    for i in range(8):
        xs[pl.ds(i * 256, 256), :] = pair_ref[pl.ds(i * 8, 8)].astype(F32).reshape(256, TC)
    for b in range(2):
        parts = []
        for k in range(16):
            r = 16 * b + k
            x = xs[pl.ds(r, C, stride=TR), :].astype(BF16)
            pc[:, pl.ds(OWN + r * TC, TC)] = x
            parts.append(x)
        pkl[b] = packed(parts, 0)
        pkr[b] = packed(parts, 8)

    pl.semaphore_wait(barrier, (nr - 1) + (na - 1) + 4)

    def rf_copy(k):
        return pltpu.make_async_remote_copy(
            rf.at[col], rf.at[col], feat_sems.at[0], feat_sems.at[1], col_peer(k), MESH
        )

    def cf_copy(k):
        return pltpu.make_async_remote_copy(
            cf.at[row], cf.at[row], feat_sems.at[2], feat_sems.at[3], row_peer(k), MESH
        )

    def start_all(copy, count, ring):
        for k in far_first(count, ring):
            copy(k).start()

    def wait_bytes(ref, sem):
        pltpu.make_async_copy(ref, ref, sem).wait()

    def wait_later(ref, send_sem, recv_sem, name):
        pending.append(lambda: wait_bytes(ref, send_sem))
        recvs[name] = lambda: wait_bytes(ref, recv_sem)

    def arrived(name):
        recvs.pop(name)()

    start_all(cf_copy, nr, nr)
    start_all(rf_copy, nc, nc)
    wait_later(rf.at[pl.ds(0, nc - 1)], feat_sems.at[0], feat_sems.at[1], "rf")
    wait_later(cf.at[pl.ds(0, nr - 1)], feat_sems.at[2], feat_sems.at[3], "cf")
    copies = halo_copies(pc, OWN, pc, pkl, pkr, hl, hr, halo_send, halo_recv)
    for i, copy in enumerate(copies):
        copy.start()
        pending.append(copy.wait_send)
        recvs[f"halo{i}"] = copy.wait_recv

    for i in range(3, 8):
        loads[i].wait()
    for i in range(8):
        xs[pl.ds(i * 256, 256), :] = cot_ref[pl.ds(i * 8, 8)].astype(F32).reshape(256, TC)
    for r in range(TR):
        c2[:, pl.ds(OWN + r * TC, TC)] = xs[pl.ds(r, C, stride=TR), :].astype(BF16)
    zeros = jnp.zeros((C, OWN), BF16)
    for part in (0, PR - D):
        c2[:, pl.ds(part * TC, OWN)] = zeros
        s2[pl.ds(3 * C, C), pl.ds(part * TC, OWN)] = zeros
    for part in (0, 1, 6, 7):
        gz[:, pl.ds(part * OWN, OWN)] = zeros
    for p in range(3):
        wf[p] = jnp.concatenate([w_ref[3 * p + q] for q in range(3)], axis=1)
        wd[p] = jnp.concatenate(
            [w_ref[3 * (2 - p) + 2 - q].astype(F32).T for q in range(3)], axis=1
        ).astype(BF16)
    pt[...] = proj_ref[...].astype(F32).T.astype(BF16)
    eye = lax.broadcasted_iota(jnp.int32, (C, C), 0) == lax.broadcasted_iota(jnp.int32, (C, C), 1)
    for src, dst in ((gain_ref, gainb), (shift_ref, shiftb)):
        column = jnp.sum(jnp.where(eye, src[...], 0.0), axis=1, keepdims=True)
        dst[...] = jnp.broadcast_to(column, (C, 2 * TC))
    arrived("rf")
    arrived("cf")

    for i in range(nr):
        cfull[pl.ds(i * cpr, cpr), :] = cf[i]
    row_full = rf[...].reshape(C, TC)
    col_full = cfull[...]
    rsend[...] = row_full.astype(BF16)
    csend[...] = col_full.astype(BF16)
    side_copies = [
        pltpu.make_async_remote_copy(
            src, dst, side_sems.at[2 * i], side_sems.at[2 * i + 1], device, MESH
        )
        for i, (src, dst, device) in enumerate(
            (
                (csend, cnear.at[1], (row, left)),
                (csend, cnear.at[0], (row, right)),
                (rsend, rnear.at[1], (up, col)),
                (rsend, rnear.at[0], (down, col)),
            )
        )
    ]
    for i, copy in enumerate(side_copies):
        copy.start()
        pending.append(copy.wait_send)
        recvs[f"side{i}"] = copy.wait_recv

    def activate(r, rows, at):
        pre = pc[:, pl.ds(r * TC, TC)].astype(F32) + rows[:, at : at + 1] + col_full
        return jnp.maximum(pre, 0.0).astype(BF16)

    def place(ref, r, x):
        ref[pl.ds(0, C), pl.ds(r * TC, TC)] = pltpu.roll(x, 8, 1)
        ref[pl.ds(C, C), pl.ds(r * TC, TC)] = x
        ref[pl.ds(2 * C, C), pl.ds(r * TC, TC)] = pltpu.roll(x, 120, 1)

    for r in range(TR):
        place(s2, D + r, activate(D + r, row_full, r))
    for i in range(4):
        arrived(f"side{i}")
    for i in range(8):
        arrived(f"halo{i}")
    above, below = rnear[0].astype(F32), rnear[1].astype(F32)
    for r in range(D):
        top = activate(r, above, TR - D + r)
        place(s2, r, jnp.where(row > 0, top, jnp.zeros_like(top)))
        bottom = activate(D + TR + r, below, r)
        place(s2, D + TR + r, jnp.where(row < nr - 1, bottom, jnp.zeros_like(bottom)))

    def spread(first, divide):
        source = lax.broadcasted_iota(jnp.int32, (TC, TC), 0)
        target = lax.broadcasted_iota(jnp.int32, (TC, TC), 1)
        wanted = target // 8 if divide else target % 8
        return (source == first + wanted).astype(BF16)

    per_row = (
        dot(rnear[0], spread(TR - 16, True)),
        dot(rsend[...], spread(0, True)),
        dot(rsend[...], spread(16, True)),
        dot(rnear[1], spread(0, True)),
    )
    per_col = (dot(cnear[0], spread(TC - 8, False)), dot(cnear[1], spread(0, False)))
    for b in range(4):
        for buffer, feature in ((hl, per_col[0]), (hr, per_col[1])):
            pre = buffer[b].astype(F32) + per_row[b] + feature
            buffer[b] = jnp.maximum(pre, 0.0).astype(BF16)
    clear_edges(hl, hr)
    set_edges(s2, hl, hr)

    gain, shift = gainb[...], shiftb[...]
    gain_sum = jnp.zeros((C, TC), F32)
    shift_sum = jnp.zeros((C, TC), F32)
    grad_copies = halo_copies(gz, 2 * OWN, gh, qkl, qkr, kl, kr, grad_send, grad_recv)

    def send_grads(which):
        for i in which:
            grad_copies[i].start()
            pending.append(grad_copies[i].wait_send)
            recvs[f"grad{i}"] = grad_copies[i].wait_recv

    for i in (0, 1, 2, 3, 12, 13, 14, 15, 4, 5, 6, 7, 8, 9, 10, 11):
        if i == 4:
            send_grads((6, 7))
        here = pl.ds(OWN + i * 256, 256)
        conv_out = sum(
            dot(wf[p], s2[pl.ds(0, 3 * C), pl.ds(p * OWN + i * 256, 256)]) for p in range(3)
        )
        back = dot(pt[...], c2[:, here])
        normed = gain * conv_out + shift
        sigma = jax.nn.sigmoid(normed)
        s2[pl.ds(3 * C, C), here] = (normed * sigma).astype(BF16)
        normed_grad = back * sigma * (1.0 + normed * (1.0 - sigma))
        product = normed_grad * conv_out
        gain_sum += product[:, :TC] + product[:, TC:]
        shift_sum += normed_grad[:, :TC] + normed_grad[:, TC:]
        gz[:, pl.ds(2 * OWN + i * 256, 256)] = (gain * normed_grad).astype(BF16)
    for b in range(2):
        parts = [
            gz[:, pl.ds(2 * OWN + (16 * b + k) * TC, TC)] for k in range(16)
        ]
        qkl[b] = packed(parts, 0)
        qkr[b] = packed(parts, 8)
    total = jnp.zeros((4 * C, 4 * C), F32)
    step = 1024
    for base in range(0, LANES, step):
        lhs = jnp.concatenate(
            [
                gz[:, pl.ds(base + 2 * OWN, step)],
                gz[:, pl.ds(base + OWN, step)],
                gz[:, pl.ds(base, step)],
                c2[:, pl.ds(base, step)],
            ],
            axis=0,
        )
        total += dot_nt(lhs, s2[:, pl.ds(base, step)])
    wacc[...] = total
    wacc[pl.ds(0, C), pl.ds(3 * C, 1)] = jnp.sum(gain_sum, axis=1, keepdims=True)
    wacc[pl.ds(0, C), pl.ds(3 * C + 1, 1)] = jnp.sum(shift_sum, axis=1, keepdims=True)

    for a in range(na):
        rs_send[a] = jnp.concatenate(
            [wacc[pl.ds(a * cr, cr), pl.ds(0, TC)], wacc[pl.ds(a * cr, cr), pl.ds(TC, TC)]], axis=0
        ).astype(BF16)

    def rs_copy(k):
        idx = lax.rem(ai + k, na)
        return pltpu.make_async_remote_copy(
            rs_send.at[idx], rs_recv.at[ai], red_sems.at[0], red_sems.at[1], a_peer(k), MESH
        )

    start_all(rs_copy, na, nc)
    wait_later(rs_send.at[pl.ds(0, na - 1)], red_sems.at[0], red_sems.at[1], "rs")
    rs_recv[ai] = rs_send[ai]

    send_grads(range(6))

    for r in range(TR):
        place(g2, D + r, gz[:, pl.ds(2 * OWN + r * TC, TC)])
    arrived("rs")
    zb[zi] = jnp.sum(rs_recv[...].astype(F32), axis=0).astype(BF16)

    def z_copy(k):
        return pltpu.make_async_remote_copy(
            zb.at[zi], zb.at[zi], red_sems.at[2], red_sems.at[3], z_peer(k), MESH
        )

    start_all(z_copy, nz, nz)
    wait_later(zb.at[pl.ds(0, nz - 1)], red_sems.at[2], red_sems.at[3], "z")
    for i in range(8):
        arrived(f"grad{i}")
    for r in range(D):
        top = gh[:, pl.ds(r * TC, TC)]
        place(g2, r, jnp.where(row > 0, top, jnp.zeros_like(top)))
        bottom = gh[:, pl.ds(OWN + TILE + r * TC, TC)]
        place(g2, D + TR + r, jnp.where(row < nr - 1, bottom, jnp.zeros_like(bottom)))
    clear_edges(kl, kr)
    set_edges(g2, kl, kr)
    root = math.sqrt(bins)
    col_sum = jnp.zeros((C, TC), F32)
    row_sum = jnp.zeros((C, TC), F32)
    for i in range(TR // 2):
        here = pl.ds(OWN + i * 256, 256)
        act_grad = sum(
            dot(wd[p], g2[:, pl.ds(p * OWN + i * 256, 256)]) for p in range(3)
        )
        active = s2[pl.ds(C, C), here].astype(F32)
        pre_grad = jnp.where(active > 0, act_grad, 0.0)
        col_sum += pre_grad[:, :TC] + pre_grad[:, TC:]
        pair_grad = pre_grad + c2[:, here].astype(F32)
        for half in range(2):
            r = 2 * i + half
            part = slice(half * TC, half * TC + TC)
            row_sum = jnp.where(
                lane == r, jnp.sum(pre_grad[:, part], axis=1, keepdims=True), row_sum
            )
            xs[pl.ds(r, C, stride=TR), :] = pair_grad[:, part]
    cacc[...] = col_sum
    for i in range(nr):
        cgs[i] = cacc[pl.ds(i * cpr, cpr), :]
    rgs[...] = row_sum.reshape(nc, cpc, TC)

    def cg_copy(k):
        idx = lax.rem(row + k, nr)
        return pltpu.make_async_remote_copy(
            cgs.at[idx], cgr.at[row], out_sems.at[0], out_sems.at[1], row_peer(k), MESH
        )

    def rg_copy(k):
        idx = lax.rem(col + k, nc)
        return pltpu.make_async_remote_copy(
            rgs.at[idx], rgr.at[col], out_sems.at[2], out_sems.at[3], col_peer(k), MESH
        )

    start_all(cg_copy, nr, nr)
    start_all(rg_copy, nc, nc)
    wait_later(cgs.at[pl.ds(0, nr - 1)], out_sems.at[0], out_sems.at[1], "cg")
    wait_later(rgs.at[pl.ds(0, nc - 1)], out_sems.at[2], out_sems.at[3], "rg")
    cgr[row] = cgs[row]
    rgr[col] = rgs[col]

    arrived("z")
    ag[ai] = (jnp.sum(zb[...].astype(F32), axis=0) * (1.0 / bins)).astype(BF16)

    def ag_copy(k):
        return pltpu.make_async_remote_copy(
            ag.at[ai], ag.at[ai], red_sems.at[4], red_sems.at[5], a_peer(k), MESH
        )

    start_all(ag_copy, na, nc)
    wait_later(ag.at[pl.ds(0, na - 1)], red_sems.at[4], red_sems.at[5], "ag")

    for i in range(8):
        pg_ref[pl.ds(i * 8, 8)] = xs[pl.ds(i * 256, 256), :].reshape(8, TR, TC).astype(BF16)

    arrived("cg")
    arrived("rg")
    colg_ref[...] = jnp.sum(cgr[...], axis=0) * (1.0 / root)
    rowg_ref[...] = jnp.sum(rgr[...], axis=0)[:, :TR] * (1.0 / root)

    arrived("ag")
    total = ag[...].astype(F32)
    low = total[:, :cr].reshape(256, TC)
    high = total[:, cr:].reshape(256, TC)
    for p in range(3):
        convg_ref[3 * p] = low[C * p : C * p + C, :C]
        convg_ref[3 * p + 1] = low[C * p : C * p + C, C:]
        convg_ref[3 * p + 2] = high[C * p : C * p + C, :C]
    projg_ref[...] = high[3 * C :, C:]
    gaing_ref[...] = jnp.sum(jnp.where(eye, high[:C, C : C + 1], 0.0), axis=0, keepdims=True)
    shiftg_ref[...] = jnp.sum(jnp.where(eye, high[:C, C + 1 : C + 2], 0.0), axis=0, keepdims=True)

    for wait in (*recvs.values(), *pending):
        wait()


def store_kernel(*refs):
    copies = [
        pltpu.make_async_copy(refs[i], refs[7 + i], refs[14].at[i]) for i in range(7)
    ]
    for copy in copies:
        copy.start()
    for copy in copies:
        copy.wait()


def shards(nr, nc, pair_in, row_feat, col_feat, cotangent, conv_weight, gain, shift, proj):
    na, nz = 4 * nc, nr // 4
    cr = 256 // na
    hbm = pl.BlockSpec(memory_space=pltpu.HBM)
    vmem = pl.BlockSpec(memory_space=pltpu.VMEM)
    scratch = dict(
        pair_ref=pltpu.VMEM((C, TR, TC), BF16),
        rowf_ref=pltpu.VMEM((C // nc, TR), BF16),
        colf_ref=pltpu.VMEM((C // nr, TC), BF16),
        cot_ref=pltpu.VMEM((C, TR, TC), BF16),
        w_ref=pltpu.VMEM((9, C, C), BF16),
        gain_ref=pltpu.VMEM((1, C), F32),
        shift_ref=pltpu.VMEM((1, C), F32),
        proj_ref=pltpu.VMEM((C, C), BF16),
        xs=pltpu.VMEM((C * TR, TC), F32),
        wf=pltpu.VMEM((3, C, 3 * C), BF16),
        pt=pltpu.VMEM((C, C), BF16),
        wd=pltpu.VMEM((3, C, 3 * C), BF16),
        gainb=pltpu.VMEM((C, 2 * TC), F32),
        shiftb=pltpu.VMEM((C, 2 * TC), F32),
        rf=pltpu.VMEM((nc, C // nc, TC), F32),
        cf=pltpu.VMEM((nr, C // nr, TC), F32),
        cfull=pltpu.VMEM((C, TC), F32),
        pc=pltpu.VMEM((C, LANES), BF16),
        rsend=pltpu.VMEM((C, TC), BF16),
        csend=pltpu.VMEM((C, TC), BF16),
        rnear=pltpu.VMEM((2, C, TC), BF16),
        cnear=pltpu.VMEM((2, C, TC), BF16),
        s2=pltpu.VMEM((4 * C, LANES), BF16),
        gh=pltpu.VMEM((C, LANES), BF16),
        c2=pltpu.VMEM((C, LANES), BF16),
        pkl=pltpu.VMEM((2, C, TC), BF16),
        pkr=pltpu.VMEM((2, C, TC), BF16),
        hl=pltpu.VMEM((4, C, TC), BF16),
        hr=pltpu.VMEM((4, C, TC), BF16),
        gz=pltpu.VMEM((C, LANES + 2 * OWN), BF16),
        g2=pltpu.VMEM((3 * C, LANES), BF16),
        qkl=pltpu.VMEM((2, C, TC), BF16),
        qkr=pltpu.VMEM((2, C, TC), BF16),
        kl=pltpu.VMEM((4, C, TC), BF16),
        kr=pltpu.VMEM((4, C, TC), BF16),
        wacc=pltpu.VMEM((4 * C, 4 * C), F32),
        rs_send=pltpu.VMEM((na, 2 * cr, TC), BF16),
        rs_recv=pltpu.VMEM((na, 2 * cr, TC), BF16),
        zb=pltpu.VMEM((nz, 2 * cr, TC), BF16),
        ag=pltpu.VMEM((na, 2 * cr, TC), BF16),
        cacc=pltpu.VMEM((C, TC), F32),
        cgs=pltpu.VMEM((nr, C // nr, TC), F32),
        cgr=pltpu.VMEM((nr, C // nr, TC), F32),
        rgs=pltpu.VMEM((nc, C // nc, TC), F32),
        rgr=pltpu.VMEM((nc, C // nc, TC), F32),
        in_sems=pltpu.SemaphoreType.DMA((8,)),
        feat_sems=pltpu.SemaphoreType.DMA((4,)),
        side_sems=pltpu.SemaphoreType.DMA((8,)),
        halo_send=pltpu.SemaphoreType.DMA((8,)),
        halo_recv=pltpu.SemaphoreType.DMA((8,)),
        grad_send=pltpu.SemaphoreType.DMA((8,)),
        grad_recv=pltpu.SemaphoreType.DMA((8,)),
        red_sems=pltpu.SemaphoreType.DMA((6,)),
        out_sems=pltpu.SemaphoreType.DMA((4,)),
    )
    shapes = (
        jax.ShapeDtypeStruct((C, TR, TC), BF16),
        jax.ShapeDtypeStruct((C // nc, TR), F32),
        jax.ShapeDtypeStruct((C // nr, TC), F32),
        jax.ShapeDtypeStruct((9, C, C), F32),
        jax.ShapeDtypeStruct((C, C), F32),
        jax.ShapeDtypeStruct((1, C), F32),
        jax.ShapeDtypeStruct((1, C), F32),
    )
    outs = pl.pallas_call(
        functools.partial(kernel, nr, nc),
        out_shape=tuple(pltpu.VMEM(shape.shape, shape.dtype) for shape in shapes),
        in_specs=[hbm] * 8,
        out_specs=(vmem,) * 7,
        scratch_shapes=list(scratch.values()),
        compiler_params=pltpu.CompilerParams(
            collective_id=0, has_side_effects=True, vmem_limit_bytes=VMEM_LIMIT
        ),
    )(
        *(
            pltpu.with_memory_space_constraint(operand, pltpu.HBM)
            for operand in (
                pair_in,
                row_feat,
                col_feat,
                cotangent,
                conv_weight,
                gain.reshape(1, C),
                shift.reshape(1, C),
                proj,
            )
        )
    )
    outs = pl.pallas_call(
        store_kernel,
        out_shape=shapes,
        in_specs=[vmem] * 7,
        out_specs=(hbm,) * 7,
        scratch_shapes=[pltpu.SemaphoreType.DMA((7,))],
        compiler_params=pltpu.CompilerParams(vmem_limit_bytes=8 * 1024 * 1024),
    )(*outs)
    return (*outs[:5], outs[5].reshape(C), outs[6].reshape(C))


def solution(mesh):
    return jax.shard_map(
        functools.partial(shards, mesh.shape["row"], mesh.shape["col"]),
        mesh=mesh,
        in_specs=(
            P(None, "row", "col"),
            P("col", "row"),
            P("row", "col"),
            P(None, "row", "col"),
            P(),
            P(),
            P(),
            P(),
        ),
        out_specs=(P(None, "row", "col"), P("col", "row"), P("row", "col"), P(), P(), P(), P()),
        check_vma=False,
    )
```

```python
import functools
import math

import jax
import jax.numpy as jnp
from jax import lax
from jax.experimental import pallas as pl
from jax.experimental.pallas import tpu as pltpu
from jax.sharding import PartitionSpec as P

C = 64
D = 8
TR = 32
TC = 128
PR = TR + 2 * D
LANES = PR * TC
OWN = D * TC
TILE = TR * TC
F32 = jnp.float32
BF16 = jnp.bfloat16
VMEM_LIMIT = 40 * 1024 * 1024
MESH = pl.DeviceIdType.MESH


def dot(a, b):
    return lax.dot_general(a, b, (((1,), (0,)), ((), ())), preferred_element_type=F32)


def dot_nt(a, b):
    return lax.dot_general(a, b, (((1,), (1,)), ((), ())), preferred_element_type=F32)


def chunking(na):
    height = 16 * (32 // na)
    return height, -(-(5 * C + 1) // height)


def kernel(
    nr,
    nc,
    pair_in,
    rowf_in,
    colf_in,
    cot_in,
    w_in,
    gain_in,
    shift_in,
    proj_in,
    pg_ref,
    rowg_ref,
    colg_ref,
    convg_ref,
    projg_ref,
    gaing_ref,
    shiftg_ref,
    pair_ref,
    rowf_ref,
    colf_ref,
    cot_ref,
    w_ref,
    gain_ref,
    shift_ref,
    proj_ref,
    xs,
    wf,
    pt,
    wd,
    gainb,
    shiftb,
    rf,
    cf,
    cfull,
    pc,
    rsend,
    csend,
    rnear,
    cnear,
    s2,
    gh,
    c2,
    pkl,
    pkr,
    hl,
    hr,
    gz,
    g2,
    qkl,
    qkr,
    kl,
    kr,
    wacc,
    rs_send,
    rs_recv,
    zb,
    ag,
    cacc,
    cgs,
    cgr,
    rgs,
    rgr,
    in_sems,
    feat_sems,
    side_sems,
    halo_send,
    halo_recv,
    grad_send,
    grad_recv,
    red_sems,
    out_sems,
):
    row = lax.axis_index("row")
    col = lax.axis_index("col")
    nz = nr // 4
    na = 4 * nc
    cpr = C // nr
    cpc = C // nc
    zi = row // 4
    ai = lax.rem(row, 4) * nc + col
    height, owners = chunking(na)
    chunk = (ai * owners + na - 1) // na
    owner = jnp.logical_and(chunk < owners, chunk * na // owners == ai)
    up, down = lax.rem(row + nr - 1, nr), lax.rem(row + 1, nr)
    left, right = lax.rem(col + nc - 1, nc), lax.rem(col + 1, nc)
    bins = TR * nr

    def row_peer(k):
        return (lax.rem(row + k, nr), col)

    def col_peer(k):
        return (row, lax.rem(col + k, nc))

    def a_peer(k):
        idx = lax.rem(ai + k, na)
        return (zi * 4 + idx // nc, lax.rem(idx, nc))

    def z_peer(k):
        return (lax.rem(zi + k, nz) * 4 + lax.rem(row, 4), col)

    def far_first(count, ring):
        return sorted(range(1, count), key=lambda k: -min(k % ring, ring - k % ring))

    barrier = pltpu.get_barrier_semaphore()

    def greet(peer, count, ring):
        for k in far_first(count, ring):
            pl.semaphore_signal(barrier, inc=1, device_id=peer(k), device_id_type=MESH)

    for dr in (up, down):
        for dc in (left, right):
            pl.semaphore_signal(barrier, inc=1, device_id=(dr, dc), device_id_type=MESH)
    greet(row_peer, nr, nr)
    greet(a_peer, na, nc)
    loads = [
        pltpu.make_async_copy(src, dst, in_sems.at[i])
        for i, (src, dst) in enumerate(
            (
                (rowf_in, rowf_ref),
                (colf_in, colf_ref),
                (pair_in, pair_ref),
                (cot_in, cot_ref),
                (w_in, w_ref),
                (proj_in, proj_ref),
                (gain_in, gain_ref),
                (shift_in, shift_ref),
            )
        )
    ]
    for load in loads:
        load.start()
    pending = []
    recvs = {}
    lane = lax.broadcasted_iota(jnp.int32, (C, TC), 1)

    def packed(parts, edge):
        result = jnp.zeros((C, TC), BF16)
        for k, x in enumerate(parts):
            shift = (8 * k + edge) % TC
            moved = pltpu.roll(x, shift, 1) if shift else x
            result = jnp.where(lane // 8 == k, moved, result)
        return result

    def halo_copies(center, base, target, lsend, rsend, lrecv, rrecv, ssem, rsem):
        plan = (
            (lsend.at[0], rrecv.at[3], (up, left)),
            (lsend.at[1], rrecv.at[0], (down, left)),
            (rsend.at[0], lrecv.at[3], (up, right)),
            (rsend.at[1], lrecv.at[0], (down, right)),
            (lsend, rrecv.at[pl.ds(1, 2)], (row, left)),
            (rsend, lrecv.at[pl.ds(1, 2)], (row, right)),
            (
                center.at[pl.ds(0, C), pl.ds(base, OWN)],
                target.at[pl.ds(0, C), pl.ds(OWN + TILE, OWN)],
                (up, col),
            ),
            (
                center.at[pl.ds(0, C), pl.ds(base + TILE - OWN, OWN)],
                target.at[pl.ds(0, C), pl.ds(0, OWN)],
                (down, col),
            ),
        )
        return [
            pltpu.make_async_remote_copy(src, dst, ssem.at[i], rsem.at[i], device, MESH)
            for i, (src, dst, device) in enumerate(plan)
        ]

    def clear_edges(lrecv, rrecv):
        @pl.when(row == 0)
        def _():
            lrecv[0] = jnp.zeros((C, TC), BF16)
            rrecv[0] = jnp.zeros((C, TC), BF16)

        @pl.when(row == nr - 1)
        def _():
            lrecv[3] = jnp.zeros((C, TC), BF16)
            rrecv[3] = jnp.zeros((C, TC), BF16)

        @pl.when(col == 0)
        def _():
            lrecv[...] = jnp.zeros_like(lrecv)

        @pl.when(col == nc - 1)
        def _():
            rrecv[...] = jnp.zeros_like(rrecv)

    def set_edges(ref, lrecv, rrecv):
        for b in range(4):
            lo, hi = lrecv[b], rrecv[b]
            for k in range(16):
                r = 16 * b + k - 8
                if not 0 <= r < PR:
                    continue
                from_left = pltpu.roll(lo, (TC - 8 * k) % TC, 1) if k else lo
                from_right = pltpu.roll(hi, 120 - 8 * k, 1) if k < 15 else hi
                at_left = ref.at[pl.ds(0, C), pl.ds(r * TC, TC)]
                at_right = ref.at[pl.ds(2 * C, C), pl.ds(r * TC, TC)]
                at_left[...] = jnp.where(lane < 8, from_left, at_left[...])
                at_right[...] = jnp.where(lane >= 120, from_right, at_right[...])

    for i in range(3):
        loads[i].wait()
    rf[col] = jnp.concatenate(
        [rowf_ref[...].astype(F32), jnp.zeros((cpc, TC - TR), F32)], axis=1
    )
    cf[row] = colf_ref[...].astype(F32)
    for i in range(8):
        xs[pl.ds(i * 256, 256), :] = pair_ref[pl.ds(i * 8, 8)].astype(F32).reshape(256, TC)
    for b in range(2):
        parts = []
        for k in range(16):
            r = 16 * b + k
            x = xs[pl.ds(r, C, stride=TR), :].astype(BF16)
            pc[:, pl.ds(OWN + r * TC, TC)] = x
            parts.append(x)
        pkl[b] = packed(parts, 0)
        pkr[b] = packed(parts, 8)

    pl.semaphore_wait(barrier, (nr - 1) + (na - 1) + 4)

    def rf_copy(k):
        return pltpu.make_async_remote_copy(
            rf.at[col], rf.at[col], feat_sems.at[0], feat_sems.at[1], col_peer(k), MESH
        )

    def cf_copy(k):
        return pltpu.make_async_remote_copy(
            cf.at[row], cf.at[row], feat_sems.at[2], feat_sems.at[3], row_peer(k), MESH
        )

    def start_all(copy, count, ring):
        for k in far_first(count, ring):
            copy(k).start()

    def wait_bytes(ref, sem):
        pltpu.make_async_copy(ref, ref, sem).wait()

    def wait_later(ref, send_sem, recv_sem, name):
        pending.append(lambda: wait_bytes(ref, send_sem))
        recvs[name] = lambda: wait_bytes(ref, recv_sem)

    def arrived(name):
        recvs.pop(name)()

    start_all(cf_copy, nr, nr)
    start_all(rf_copy, nc, nc)
    wait_later(rf.at[pl.ds(0, nc - 1)], feat_sems.at[0], feat_sems.at[1], "rf")
    wait_later(cf.at[pl.ds(0, nr - 1)], feat_sems.at[2], feat_sems.at[3], "cf")
    copies = halo_copies(pc, OWN, pc, pkl, pkr, hl, hr, halo_send, halo_recv)
    for i, copy in enumerate(copies):
        copy.start()
        pending.append(copy.wait_send)
        recvs[f"halo{i}"] = copy.wait_recv

    for i in range(3, 8):
        loads[i].wait()
    for i in range(8):
        xs[pl.ds(i * 256, 256), :] = cot_ref[pl.ds(i * 8, 8)].astype(F32).reshape(256, TC)
    for r in range(TR):
        c2[:, pl.ds(OWN + r * TC, TC)] = xs[pl.ds(r, C, stride=TR), :].astype(BF16)
    zeros = jnp.zeros((C, OWN), BF16)
    for part in (0, PR - D):
        c2[:, pl.ds(part * TC, OWN)] = zeros
        s2[pl.ds(3 * C, C), pl.ds(part * TC, OWN)] = zeros
    for part in (0, 1, 6, 7):
        gz[:, pl.ds(part * OWN, OWN)] = zeros
    for p in range(3):
        wf[p] = jnp.concatenate([w_ref[3 * p + q] for q in range(3)], axis=1)
        wd[p] = jnp.concatenate(
            [w_ref[3 * (2 - p) + 2 - q].astype(F32).T for q in range(3)], axis=1
        ).astype(BF16)
    pt[...] = proj_ref[...].astype(F32).T.astype(BF16)
    eye = lax.broadcasted_iota(jnp.int32, (C, C), 0) == lax.broadcasted_iota(jnp.int32, (C, C), 1)
    for src, dst in ((gain_ref, gainb), (shift_ref, shiftb)):
        column = jnp.sum(jnp.where(eye, src[...], 0.0), axis=1, keepdims=True)
        dst[...] = jnp.broadcast_to(column, (C, 2 * TC))
    arrived("rf")
    arrived("cf")

    for i in range(nr):
        cfull[pl.ds(i * cpr, cpr), :] = cf[i]
    row_full = rf[...].reshape(C, TC)
    col_full = cfull[...]
    rsend[...] = row_full.astype(BF16)
    csend[...] = col_full.astype(BF16)
    side_copies = [
        pltpu.make_async_remote_copy(
            src, dst, side_sems.at[2 * i], side_sems.at[2 * i + 1], device, MESH
        )
        for i, (src, dst, device) in enumerate(
            (
                (csend, cnear.at[1], (row, left)),
                (csend, cnear.at[0], (row, right)),
                (rsend, rnear.at[1], (up, col)),
                (rsend, rnear.at[0], (down, col)),
            )
        )
    ]
    for i, copy in enumerate(side_copies):
        copy.start()
        pending.append(copy.wait_send)
        recvs[f"side{i}"] = copy.wait_recv

    def activate(r, rows, at):
        pre = pc[:, pl.ds(r * TC, TC)].astype(F32) + rows[:, at : at + 1] + col_full
        return jnp.maximum(pre, 0.0).astype(BF16)

    def place(ref, r, x):
        ref[pl.ds(0, C), pl.ds(r * TC, TC)] = pltpu.roll(x, 8, 1)
        ref[pl.ds(C, C), pl.ds(r * TC, TC)] = x
        ref[pl.ds(2 * C, C), pl.ds(r * TC, TC)] = pltpu.roll(x, 120, 1)

    for r in range(TR):
        place(s2, D + r, activate(D + r, row_full, r))
    for i in range(4):
        arrived(f"side{i}")
    for i in range(8):
        arrived(f"halo{i}")
    above, below = rnear[0].astype(F32), rnear[1].astype(F32)
    for r in range(D):
        top = activate(r, above, TR - D + r)
        place(s2, r, jnp.where(row > 0, top, jnp.zeros_like(top)))
        bottom = activate(D + TR + r, below, r)
        place(s2, D + TR + r, jnp.where(row < nr - 1, bottom, jnp.zeros_like(bottom)))

    def spread(first, divide):
        source = lax.broadcasted_iota(jnp.int32, (TC, TC), 0)
        target = lax.broadcasted_iota(jnp.int32, (TC, TC), 1)
        wanted = target // 8 if divide else target % 8
        return (source == first + wanted).astype(BF16)

    per_row = (
        dot(rnear[0], spread(TR - 16, True)),
        dot(rsend[...], spread(0, True)),
        dot(rsend[...], spread(16, True)),
        dot(rnear[1], spread(0, True)),
    )
    per_col = (dot(cnear[0], spread(TC - 8, False)), dot(cnear[1], spread(0, False)))
    for b in range(4):
        for buffer, feature in ((hl, per_col[0]), (hr, per_col[1])):
            pre = buffer[b].astype(F32) + per_row[b] + feature
            buffer[b] = jnp.maximum(pre, 0.0).astype(BF16)
    clear_edges(hl, hr)
    set_edges(s2, hl, hr)

    gain, shift = gainb[...], shiftb[...]
    gain_sum = jnp.zeros((C, TC), F32)
    shift_sum = jnp.zeros((C, TC), F32)
    grad_copies = halo_copies(gz, 2 * OWN, gh, qkl, qkr, kl, kr, grad_send, grad_recv)

    def send_grads(which):
        for i in which:
            grad_copies[i].start()
            pending.append(grad_copies[i].wait_send)
            recvs[f"grad{i}"] = grad_copies[i].wait_recv

    def weights(part):
        base = part * OWN
        lhs = jnp.concatenate(
            [
                gz[:, pl.ds(base + 2 * OWN, OWN)],
                gz[:, pl.ds(base + OWN, OWN)],
                gz[:, pl.ds(base, OWN)],
                c2[:, pl.ds(base, OWN)],
            ],
            axis=0,
        )
        return dot_nt(lhs, s2[:, pl.ds(base, OWN)])

    sums = []
    for i in (0, 1, 2, 3, 12, 13, 14, 15, 4, 5, 6, 7, 8, 9, 10, 11):
        if i == 4:
            send_grads((6, 7))
            sums = [weights(0) + weights(5)]
        if i == 8:
            sums = [sums[0] + weights(1)]
        here = pl.ds(OWN + i * 256, 256)
        conv_out = sum(
            dot(wf[p], s2[pl.ds(0, 3 * C), pl.ds(p * OWN + i * 256, 256)]) for p in range(3)
        )
        back = dot(pt[...], c2[:, here])
        normed = gain * conv_out + shift
        sigma = jax.nn.sigmoid(normed)
        s2[pl.ds(3 * C, C), here] = (normed * sigma).astype(BF16)
        normed_grad = back * sigma * (1.0 + normed * (1.0 - sigma))
        product = normed_grad * conv_out
        gain_sum += product[:, :TC] + product[:, TC:]
        shift_sum += normed_grad[:, :TC] + normed_grad[:, TC:]
        gz[:, pl.ds(2 * OWN + i * 256, 256)] = (gain * normed_grad).astype(BF16)
    for b in range(2):
        parts = [
            gz[:, pl.ds(2 * OWN + (16 * b + k) * TC, TC)] for k in range(16)
        ]
        qkl[b] = packed(parts, 0)
        qkr[b] = packed(parts, 8)
    wacc[...] = sums[0] + weights(2) + weights(3) + weights(4)
    sides = [
        jnp.sum(jnp.where(eye, jnp.sum(part, axis=1, keepdims=True), 0.0), axis=0, keepdims=True)
        for part in (gain_sum, shift_sum)
    ]
    low, high = wacc[:, :TC], wacc[:, TC:]
    left_half = lane[:32] < C
    pieces = [low[i * 32 : i * 32 + 32] for i in range(6)]
    for i in range(3):
        first, second = high[i * 32 : i * 32 + 32], high[96 + i * 32 : 128 + i * 32]
        pieces.append(jnp.where(left_half, first, pltpu.roll(second, C, 1)))
    pieces.append(jnp.where(left_half, pltpu.roll(high[192:224], C, 1), high[224:256]))
    pieces.append(
        jnp.broadcast_to(jnp.concatenate(sides, axis=1), (height * owners - 5 * C, TC))
    )
    packed_sums = jnp.concatenate(pieces, axis=0).astype(BF16)
    for i in range(owners):
        rs_send[i] = packed_sums[i * height : i * height + height]

    def a_device(idx):
        return (zi * 4 + idx // nc, lax.rem(idx, nc))

    def rs_copy(k):
        part = lax.rem(chunk + k, owners)
        return pltpu.make_async_remote_copy(
            rs_send.at[part],
            rs_recv.at[ai],
            red_sems.at[0],
            red_sems.at[1],
            a_device(part * na // owners),
            MESH,
        )

    start_all(rs_copy, owners, owners)

    @pl.when(jnp.logical_not(owner))
    def _():
        rs_copy(0).start()

    @pl.when(owner)
    def _():
        rs_recv[ai] = rs_send[chunk]

    def wait_if_owner(ref, sem, when_owner, otherwise):
        @pl.when(owner)
        def _():
            wait_bytes(ref.at[pl.ds(0, when_owner)], sem)

        if otherwise:
            @pl.when(jnp.logical_not(owner))
            def _():
                wait_bytes(ref.at[pl.ds(0, otherwise)], sem)

    pending.append(lambda: wait_if_owner(rs_send, red_sems.at[0], owners - 1, owners))

    send_grads(range(6))

    for r in range(TR):
        place(g2, D + r, gz[:, pl.ds(2 * OWN + r * TC, TC)])
    def z_copy(k):
        return pltpu.make_async_remote_copy(
            zb.at[zi], zb.at[zi], red_sems.at[2], red_sems.at[3], z_peer(k), MESH
        )

    @pl.when(owner)
    def _():
        wait_bytes(rs_recv.at[pl.ds(0, na - 1)], red_sems.at[1])
        zb[zi] = jnp.sum(rs_recv[...].astype(F32), axis=0).astype(BF16)
        start_all(z_copy, nz, nz)

    pending.append(lambda: wait_if_owner(zb, red_sems.at[2], nz - 1, 0))

    for i in range(8):
        arrived(f"grad{i}")
    for r in range(D):
        top = gh[:, pl.ds(r * TC, TC)]
        place(g2, r, jnp.where(row > 0, top, jnp.zeros_like(top)))
        bottom = gh[:, pl.ds(OWN + TILE + r * TC, TC)]
        place(g2, D + TR + r, jnp.where(row < nr - 1, bottom, jnp.zeros_like(bottom)))
    clear_edges(kl, kr)
    set_edges(g2, kl, kr)
    root = math.sqrt(bins)
    col_sum = jnp.zeros((C, TC), F32)
    row_sum = jnp.zeros((C, TC), F32)
    for i in range(TR // 2):
        here = pl.ds(OWN + i * 256, 256)
        act_grad = sum(
            dot(wd[p], g2[:, pl.ds(p * OWN + i * 256, 256)]) for p in range(3)
        )
        active = s2[pl.ds(C, C), here].astype(F32)
        pre_grad = jnp.where(active > 0, act_grad, 0.0)
        col_sum += pre_grad[:, :TC] + pre_grad[:, TC:]
        pair_grad = pre_grad + c2[:, here].astype(F32)
        for half in range(2):
            r = 2 * i + half
            part = slice(half * TC, half * TC + TC)
            row_sum = jnp.where(
                lane == r, jnp.sum(pre_grad[:, part], axis=1, keepdims=True), row_sum
            )
            xs[pl.ds(r, C, stride=TR), :] = pair_grad[:, part]
    cacc[...] = col_sum
    for i in range(nr):
        cgs[i] = cacc[pl.ds(i * cpr, cpr), :]
    rgs[...] = row_sum.reshape(nc, cpc, TC)

    def cg_copy(k):
        idx = lax.rem(row + k, nr)
        return pltpu.make_async_remote_copy(
            cgs.at[idx], cgr.at[row], out_sems.at[0], out_sems.at[1], row_peer(k), MESH
        )

    def rg_copy(k):
        idx = lax.rem(col + k, nc)
        return pltpu.make_async_remote_copy(
            rgs.at[idx], rgr.at[col], out_sems.at[2], out_sems.at[3], col_peer(k), MESH
        )

    start_all(cg_copy, nr, nr)
    start_all(rg_copy, nc, nc)
    wait_later(cgs.at[pl.ds(0, nr - 1)], out_sems.at[0], out_sems.at[1], "cg")
    wait_later(rgs.at[pl.ds(0, nc - 1)], out_sems.at[2], out_sems.at[3], "rg")
    cgr[row] = cgs[row]
    rgr[col] = rgs[col]

    def ag_copy(k):
        return pltpu.make_async_remote_copy(
            ag.at[chunk], ag.at[chunk], red_sems.at[4], red_sems.at[5], a_peer(k), MESH
        )

    @pl.when(owner)
    def _():
        wait_bytes(zb.at[pl.ds(0, nz - 1)], red_sems.at[3])
        ag[chunk] = (jnp.sum(zb[...].astype(F32), axis=0) * (1.0 / bins)).astype(BF16)
        start_all(ag_copy, na, nc)

    pending.append(lambda: wait_if_owner(rs_recv, red_sems.at[4], na - 1, 0))

    for i in range(8):
        pg_ref[pl.ds(i * 8, 8)] = xs[pl.ds(i * 256, 256), :].reshape(8, TR, TC).astype(BF16)

    arrived("cg")
    arrived("rg")
    colg_ref[...] = jnp.sum(cgr[...], axis=0) * (1.0 / root)
    rowg_ref[...] = jnp.sum(rgr[...], axis=0)[:, :TR] * (1.0 / root)

    wait_if_owner(ag, red_sems.at[5], owners - 1, owners)
    total = ag[...].astype(F32).reshape(height * owners, TC)
    for p in range(3):
        convg_ref[3 * p] = total[C * p : C * p + C, :C]
        convg_ref[3 * p + 1] = total[C * p : C * p + C, C:]
    high = total[3 * C : 3 * C + 96]
    convg_ref[2] = high[:C, :C]
    convg_ref[5, pl.ds(0, 32)] = high[C:, :C]
    convg_ref[5, pl.ds(32, 32)] = high[:32, C:]
    convg_ref[8] = high[32:, C:]
    projg_ref[pl.ds(0, 32)] = total[288:320, :C]
    projg_ref[pl.ds(32, 32)] = total[288:320, C:]
    gaing_ref[...] = total[320:321, :C]
    shiftg_ref[...] = total[320:321, C:]

    for wait in (*recvs.values(), *pending):
        wait()


def store_kernel(*refs):
    copies = [
        pltpu.make_async_copy(refs[i], refs[7 + i], refs[14].at[i]) for i in range(7)
    ]
    for copy in copies:
        copy.start()
    for copy in copies:
        copy.wait()


def shards(nr, nc, pair_in, row_feat, col_feat, cotangent, conv_weight, gain, shift, proj):
    na, nz = 4 * nc, nr // 4
    height, owners = chunking(na)
    hbm = pl.BlockSpec(memory_space=pltpu.HBM)
    vmem = pl.BlockSpec(memory_space=pltpu.VMEM)
    scratch = dict(
        pair_ref=pltpu.VMEM((C, TR, TC), BF16),
        rowf_ref=pltpu.VMEM((C // nc, TR), BF16),
        colf_ref=pltpu.VMEM((C // nr, TC), BF16),
        cot_ref=pltpu.VMEM((C, TR, TC), BF16),
        w_ref=pltpu.VMEM((9, C, C), BF16),
        gain_ref=pltpu.VMEM((1, C), F32),
        shift_ref=pltpu.VMEM((1, C), F32),
        proj_ref=pltpu.VMEM((C, C), BF16),
        xs=pltpu.VMEM((C * TR, TC), F32),
        wf=pltpu.VMEM((3, C, 3 * C), BF16),
        pt=pltpu.VMEM((C, C), BF16),
        wd=pltpu.VMEM((3, C, 3 * C), BF16),
        gainb=pltpu.VMEM((C, 2 * TC), F32),
        shiftb=pltpu.VMEM((C, 2 * TC), F32),
        rf=pltpu.VMEM((nc, C // nc, TC), F32),
        cf=pltpu.VMEM((nr, C // nr, TC), F32),
        cfull=pltpu.VMEM((C, TC), F32),
        pc=pltpu.VMEM((C, LANES), BF16),
        rsend=pltpu.VMEM((C, TC), BF16),
        csend=pltpu.VMEM((C, TC), BF16),
        rnear=pltpu.VMEM((2, C, TC), BF16),
        cnear=pltpu.VMEM((2, C, TC), BF16),
        s2=pltpu.VMEM((4 * C, LANES), BF16),
        gh=pltpu.VMEM((C, LANES), BF16),
        c2=pltpu.VMEM((C, LANES), BF16),
        pkl=pltpu.VMEM((2, C, TC), BF16),
        pkr=pltpu.VMEM((2, C, TC), BF16),
        hl=pltpu.VMEM((4, C, TC), BF16),
        hr=pltpu.VMEM((4, C, TC), BF16),
        gz=pltpu.VMEM((C, LANES + 2 * OWN), BF16),
        g2=pltpu.VMEM((3 * C, LANES), BF16),
        qkl=pltpu.VMEM((2, C, TC), BF16),
        qkr=pltpu.VMEM((2, C, TC), BF16),
        kl=pltpu.VMEM((4, C, TC), BF16),
        kr=pltpu.VMEM((4, C, TC), BF16),
        wacc=pltpu.VMEM((4 * C, 4 * C), F32),
        rs_send=pltpu.VMEM((owners, height, TC), BF16),
        rs_recv=pltpu.VMEM((na, height, TC), BF16),
        zb=pltpu.VMEM((nz, height, TC), BF16),
        ag=pltpu.VMEM((owners, height, TC), BF16),
        cacc=pltpu.VMEM((C, TC), F32),
        cgs=pltpu.VMEM((nr, C // nr, TC), F32),
        cgr=pltpu.VMEM((nr, C // nr, TC), F32),
        rgs=pltpu.VMEM((nc, C // nc, TC), F32),
        rgr=pltpu.VMEM((nc, C // nc, TC), F32),
        in_sems=pltpu.SemaphoreType.DMA((8,)),
        feat_sems=pltpu.SemaphoreType.DMA((4,)),
        side_sems=pltpu.SemaphoreType.DMA((8,)),
        halo_send=pltpu.SemaphoreType.DMA((8,)),
        halo_recv=pltpu.SemaphoreType.DMA((8,)),
        grad_send=pltpu.SemaphoreType.DMA((8,)),
        grad_recv=pltpu.SemaphoreType.DMA((8,)),
        red_sems=pltpu.SemaphoreType.DMA((6,)),
        out_sems=pltpu.SemaphoreType.DMA((4,)),
    )
    shapes = (
        jax.ShapeDtypeStruct((C, TR, TC), BF16),
        jax.ShapeDtypeStruct((C // nc, TR), F32),
        jax.ShapeDtypeStruct((C // nr, TC), F32),
        jax.ShapeDtypeStruct((9, C, C), F32),
        jax.ShapeDtypeStruct((C, C), F32),
        jax.ShapeDtypeStruct((1, C), F32),
        jax.ShapeDtypeStruct((1, C), F32),
    )
    outs = pl.pallas_call(
        functools.partial(kernel, nr, nc),
        out_shape=tuple(pltpu.VMEM(shape.shape, shape.dtype) for shape in shapes),
        in_specs=[hbm] * 8,
        out_specs=(vmem,) * 7,
        scratch_shapes=list(scratch.values()),
        compiler_params=pltpu.CompilerParams(
            collective_id=0, has_side_effects=True, vmem_limit_bytes=VMEM_LIMIT
        ),
    )(
        *(
            pltpu.with_memory_space_constraint(operand, pltpu.HBM)
            for operand in (
                pair_in,
                row_feat,
                col_feat,
                cotangent,
                conv_weight,
                gain.reshape(1, C),
                shift.reshape(1, C),
                proj,
            )
        )
    )
    outs = pl.pallas_call(
        store_kernel,
        out_shape=shapes,
        in_specs=[vmem] * 7,
        out_specs=(hbm,) * 7,
        scratch_shapes=[pltpu.SemaphoreType.DMA((7,))],
        compiler_params=pltpu.CompilerParams(vmem_limit_bytes=8 * 1024 * 1024),
    )(*outs)
    return (*outs[:5], outs[5].reshape(C), outs[6].reshape(C))


def solution(mesh):
    return jax.shard_map(
        functools.partial(shards, mesh.shape["row"], mesh.shape["col"]),
        mesh=mesh,
        in_specs=(
            P(None, "row", "col"),
            P("col", "row"),
            P("row", "col"),
            P(None, "row", "col"),
            P(),
            P(),
            P(),
            P(),
        ),
        out_specs=(P(None, "row", "col"), P("col", "row"), P("row", "col"), P(), P(), P(), P()),
        check_vma=False,
    )
```
